512 devices in a mesh: leaf: 512 (over y, z, x, core).
Axes of the slice: x: 4, y: 8, z: 8, core: 2. Of those that a mesh axis runs over, the one named last changes fastest.
Arguments:
- points: float32 [3, 2097152], P(None, 'leaf'), may hold values from 0 to 1
- charges: float32 [16, 2097152], P(None, 'leaf'), may hold values from -6 to 6
- basis: float32 [64, 2097152], P(None, 'leaf'), may hold values from -0.5 to 0.5
- transfer: float32 [2, 64, 64], replicated, may hold values from -0.75 to 0.75
- near_list: int32 [12, 16384], P(None, 'leaf'), may hold values from 0 to 16383, as said below
- coupling_list: int32 [4, 32760], replicated, may hold values from 0 to 16383, as said below
- ordering: int32 [2097152], P('leaf'), may hold values from 0 to 127, as said below
Outputs:
- potential: float32 [16, 2097152], P(None, 'leaf')
The draws below stay inside these ranges and needn't reach their ends.
Inputs may be any that keep to these rules, and one draw needn't show every extreme that they name: `near_list`: entry 0 of leaf b is b; the 12 entries of a leaf are distinct and each is (b + w) mod 16384 with 1 <= |w| <= 32. `coupling_list`: column 2 * 16384 - 2 n + t, for a level with n = 16384 >> l clusters (l from 0 while n >= 8), lists clusters (t + o) mod n of that level with each o one of 2, 3, -3, -2; entries may repeat. `ordering`: the 128 entries of each leaf are a permutation of 0 to 127.
All inputs are finite; a program needn't handle non-finite values.
Results may differ from the reference program's by a relative error of at most 0.0003.
Values sent between devices are 32-bit elements; how exact they have to be, the bound alone decides.
No kernel may reach another device: no remote copies, remote signals or barrier semaphores. Data moves between devices by JAX's collectives and lax.ppermute only.
A program may use at most 128 MiB of HBM per device.

```python
import math
import jax
import jax.numpy as jnp
from jax import lax

LEAF = 128
RHS = 16
ORDER = 4
RANK = 64
NEAR = 12
CPL = 4
LEAF_DEV = 32
LOG_DEV = 5
UPPER = 6
NL = 16384
NPTS = 2097152
NODES = 32760


def draw_near_list(key, part):
    key = jax.random.fold_in(key, 11)
    window = 2 * LEAF_DEV
    steps_pool = jnp.concatenate([jnp.arange(1, LEAF_DEV + 1, dtype=jnp.int32), -jnp.arange(1, LEAF_DEV + 1, dtype=jnp.int32)])
    scores = jax.random.randint(key, (NL, window), 0, 1 << 20, dtype=jnp.int32) * window + jnp.arange(window, dtype=jnp.int32)[None, :]
    picked = jnp.argsort(scores, axis=1)[:, :NEAR - 1]
    offsets = jnp.take(steps_pool, picked)
    leaf_ids = jnp.arange(NL, dtype=jnp.int32)[:, None]
    neighbours = jnp.mod(leaf_ids + offsets, NL)
    return jnp.concatenate([leaf_ids, neighbours], axis=1).T.astype(jnp.int32)


def draw_coupling_list(key, part):
    key = jax.random.fold_in(key, 23)
    top_level = NL.bit_length() - 1 - 3
    targets = jnp.concatenate([jnp.arange(NL >> level_id, dtype=jnp.int32) for level_id in range(top_level + 1)])
    widths = jnp.concatenate([jnp.full((NL >> level_id,), NL >> level_id, dtype=jnp.int32) for level_id in range(top_level + 1)])
    picks = jax.random.randint(key, (CPL, NODES), 0, 4, dtype=jnp.int32)
    shift_table = jnp.array([2, 3, -3, -2], dtype=jnp.int32)
    shifts = jnp.take(shift_table, picks)
    return jnp.mod(targets[None, :] + shifts, widths[None, :]).astype(jnp.int32)


def draw_ordering(key, part):
    key = jax.random.fold_in(key, 37)
    scores = jax.random.randint(key, (NL, LEAF), 0, 1 << 20, dtype=jnp.int32) * LEAF + jnp.arange(LEAF, dtype=jnp.int32)[None, :]
    return jnp.argsort(scores, axis=1).astype(jnp.int32).reshape(NPTS)


def levels(own_key, extent, pieces, smallest, largest):
    def one(position, parts):
        heights = jax.random.uniform(jax.random.fold_in(jax.random.fold_in(own_key, 6), position), (parts,), jnp.float32, smallest / len(pieces), largest / len(pieces))
        return jnp.repeat(jnp.exp(heights), extent[position] // parts).reshape((-1,) + (1,) * (len(extent) - position - 1))

    gain = one(*pieces[0])
    for cut in pieces[1:]:
        gain = gain * one(*cut)
    return gain


def centred(rng, extent, width, bound, cuts=(), kind=jnp.bfloat16):
    entries = width * jax.random.normal(rng, extent, jnp.float32)
    if cuts:
        entries = entries * levels(rng, extent, cuts, -0.22, 0.18)
    return jnp.clip(entries, -bound, bound).astype(kind)


def setup_inputs(seed: int = 0) -> dict:
    keys = jax.random.split(jax.random.key(seed), 8)
    points = jnp.clip(1.0 * jax.random.uniform(keys[0], (3, NPTS), jnp.float32) ** levels(keys[0], (3, NPTS), ((1, 512),), -0.2, 0.2), 0.0, 1.0)
    charges = centred(keys[1], (RHS, NPTS), 1.0, 6.0, ((1, 512),), jnp.float32)
    basis = centred(keys[2], (RANK, NPTS), LEAF ** -0.5, 0.5, ((1, 512),), jnp.float32)
    transfer = centred(keys[3], (2, RANK, RANK), RANK ** -0.5, 0.75, (), jnp.float32)
    near_list = draw_near_list(jax.random.fold_in(keys[7], 71), 0)
    coupling_list = draw_coupling_list(jax.random.fold_in(keys[7], 71), 0)
    ordering = draw_ordering(jax.random.fold_in(keys[7], 71), 0)
    return dict(points=points, charges=charges, basis=basis, transfer=transfer, near_list=near_list, coupling_list=coupling_list, ordering=ordering)


HIGHEST = lax.Precision.HIGHEST
OFFSETS = (2, 3, -3, -2)
DELTA = 0.05
PROXY = 0.35

def unit_nodes(node_order):
    counter = jnp.arange(node_order, dtype=jnp.float32)
    cheb_nodes = jnp.cos((2.0 * counter + 1.0) * (math.pi / (2.0 * node_order)))
    coord_one = jnp.repeat(cheb_nodes, node_order * node_order)
    coord_two = jnp.tile(jnp.repeat(cheb_nodes, node_order), node_order)
    coord_three = jnp.tile(cheb_nodes, node_order * node_order)
    return jnp.stack([coord_one, coord_two, coord_three])

def coupling_blocks(node_order):
    proxies = unit_nodes(node_order) * PROXY
    stacked = []
    for shift_by in OFFSETS:
        moved = proxies + jnp.array([float(shift_by), 0.0, 0.0], dtype=jnp.float32)[:, None]
        difference = proxies[:, :, None] - moved[:, None, :]
        distance = jnp.sqrt(lax.optimization_barrier(jnp.sum(difference * difference, axis=0)))
        stacked.append(0.25 / math.pi / distance)
    return jnp.stack(stacked)

def apply_up(left_part, right_part, transfer):
    return jnp.einsum('...ra,ab->...rb', left_part, transfer[0], precision=HIGHEST) + jnp.einsum('...ra,ab->...rb', right_part, transfer[1], precision=HIGHEST)

def apply_down(parent, matrix):
    return jnp.einsum('...rb,ab->...ra', parent, matrix, precision=HIGHEST)

def offset_counts(row_ids, targets, clusters):
    relative = jnp.mod(row_ids - targets[None, :], clusters)
    return [lax.optimization_barrier(jnp.sum((relative == shift_by % clusters).astype(jnp.float32), axis=0)) for shift_by in OFFSETS]

def combine(candidates, counts, blocks, level_id):
    summed = jnp.zeros(candidates[0].shape, jnp.float32)
    for slot_id in range(len(OFFSETS)):
        product = jnp.einsum('nrb,ab->nra', candidates[slot_id], blocks[slot_id], precision=HIGHEST)
        summed = summed + counts[slot_id][:, None, None] * product
    return summed * 0.5 ** level_id

def wrapped(delta_ids, total_leaves):
    half_cycle = total_leaves // 2
    return jnp.mod(delta_ids + half_cycle, total_leaves) - half_cycle

def near_group(targets, sources, offsets, leaf_pitch):
    shift_x = offsets.astype(jnp.float32) * leaf_pitch
    dist_sq = jnp.full((sources.shape[0], sources.shape[1], targets.shape[2], sources.shape[3]), DELTA * DELTA, jnp.float32)
    for axis_id in range(3):
        source_axis = sources[:, :, axis_id, :]
        if axis_id == 0:
            source_axis = source_axis + shift_x[:, :, None]
        difference = targets[axis_id][:, None, :, None] - source_axis[:, :, None, :]
        dist_sq = dist_sq + difference * difference
    kernel = lax.rsqrt(dist_sq) * (0.25 / math.pi)
    return jnp.einsum('gkij,gkrj->rgi', kernel, sources[:, :, 3:, :], precision=HIGHEST)

def reference(points, charges, basis, transfer, near_list, coupling_list, ordering):
    leaves = NL
    top_level = LOG_DEV + UPPER
    leaf_pitch = 1.0 / LEAF_DEV
    permuted_ids = ordering.reshape(leaves, LEAF)
    inverse_ids = jnp.argsort(permuted_ids, axis=1).astype(jnp.int32)

    def to_tree(values):
        shaped = values.reshape(values.shape[0], leaves, LEAF)
        return jnp.take_along_axis(shaped, permuted_ids[None], axis=2)
    data = jnp.concatenate([to_tree(points), to_tree(charges)], axis=0)

    def near_block(group_id):
        leaf_ids = group_id * 4 + jnp.arange(4, dtype=jnp.int32)
        source_ids = jnp.take(near_list, leaf_ids, axis=1).T
        offsets = wrapped(source_ids - leaf_ids[:, None], leaves)
        sources = jnp.transpose(jnp.take(data, source_ids, axis=1), (1, 2, 0, 3))
        targets = jnp.take(data[:3], leaf_ids, axis=1)
        return near_group(targets, sources, offsets, leaf_pitch)
    near_part = lax.map(near_block, jnp.arange(leaves // 4, dtype=jnp.int32))
    near_part = jnp.transpose(near_part, (1, 0, 2, 3)).reshape(RHS, leaves, LEAF)
    basis_leaf = basis.reshape(RANK, leaves, LEAF)
    current = jnp.einsum('anl,rnl->nra', basis_leaf, data[3:], precision=HIGHEST)
    blocks = coupling_blocks(ORDER)
    local_terms = []
    for level_id in range(top_level + 1):
        clusters = leaves >> level_id
        start = 2 * leaves - 2 * clusters
        row_ids = coupling_list[:, start:start + clusters]
        counts = offset_counts(row_ids, jnp.arange(clusters, dtype=jnp.int32), clusters)
        candidates = [jnp.roll(current, -shift_by, axis=0) for shift_by in OFFSETS]
        local_terms.append(combine(candidates, counts, blocks, level_id))
        if level_id < top_level:
            paired = current.reshape(clusters // 2, 2, RHS, RANK)
            current = apply_up(paired[:, 0], paired[:, 1], transfer)
    summed_down = local_terms[top_level]
    for level_id in range(top_level, 0, -1):
        child = local_terms[level_id - 1].reshape(-1, 2, RHS, RANK)
        first_child = child[:, 0] + apply_down(summed_down, transfer[0])
        second_child = child[:, 1] + apply_down(summed_down, transfer[1])
        summed_down = jnp.stack([first_child, second_child], axis=1).reshape(-1, RHS, RANK)
    far_part = jnp.einsum('nra,anl->rnl', summed_down, basis_leaf, precision=HIGHEST)
    tree_total = near_part + far_part
    return jnp.take_along_axis(tree_total, inverse_ids[None], axis=2).reshape(RHS, NPTS)
```

```python
import math

import jax
import jax.numpy as jnp
import numpy as np
from jax import lax
from jax.experimental import pallas as pl
from jax.experimental.pallas import tpu as pltpu
from jax.sharding import PartitionSpec as P

ORDER = 4
OFFSETS = (2, 3, -3, -2)
DELTA = 0.05
PROXY = 0.35
HIGHEST = lax.Precision.HIGHEST
GROUP = 16
LANES = 128
VMEM_BYTES = 50 * 1024 * 1024


def coupling_stack():
    nodes = np.cos((2.0 * np.arange(ORDER) + 1.0) * (math.pi / (2.0 * ORDER)))
    grid = np.stack(np.meshgrid(nodes, nodes, nodes, indexing="ij")).reshape(3, -1) * PROXY
    stacked = []
    for shift_by in OFFSETS:
        moved = grid + np.array([float(shift_by), 0.0, 0.0])[:, None]
        difference = grid[:, :, None] - moved[:, None, :]
        stacked.append((0.25 / math.pi / np.sqrt((difference**2).sum(0))).T)
    table = np.concatenate(stacked, axis=0)
    return np.concatenate([table, table], axis=1).astype(np.float32)


def dot(left, right):
    return lax.dot_general(
        left, right, (((1,), (0,)), ((), ())), precision=HIGHEST, preferred_element_type=jnp.float32
    )


def dot_t(left, right):
    return lax.dot_general(
        left, right, (((1,), (1,)), ((), ())), precision=HIGHEST, preferred_element_type=jnp.float32
    )


def first_half(shape):
    return lax.broadcasted_iota(jnp.int32, shape, len(shape) - 1) < LANES // 2


def packed(left, right):
    return jnp.where(first_half(left.shape), left, right)


def unpacked(both):
    turned = pltpu.roll(both, LANES // 2, 1)
    return packed(both, turned), packed(turned, both)


def twice(matrix):
    return jnp.concatenate([matrix, matrix], axis=1)


def up_matrix(transfer_ref):
    return jnp.concatenate([twice(transfer_ref[0]), twice(transfer_ref[1])], axis=0)


def up(values, matrix):
    count, rows, lanes = values.shape
    paired = values.reshape(count // 2, 2, rows, lanes)
    both = packed(paired[:, 0], paired[:, 1]).reshape(count // 2 * rows, lanes)
    return dot(both, matrix).reshape(count // 2, rows, lanes)


def down(parents, transfer_ref, half):
    count, rows, lanes = parents.shape
    matrix = transfer_ref[half]
    doubled = jnp.concatenate([matrix, matrix], axis=0)
    flat = parents.reshape(count * rows, lanes)[:, : lanes // 2]
    return dot_t(flat, doubled).reshape(count, rows, lanes)


def down_all(parents, transfer_ref):
    count, rows, lanes = parents.shape
    children = jnp.stack(
        [down(parents, transfer_ref, 0), down(parents, transfer_ref, 1)], axis=1
    )
    return children.reshape(2 * count, rows, lanes)


def level_starts(total_leaves, levels):
    return [2 * total_leaves - 2 * (total_leaves >> level) for level in range(levels)]


def prepare_kernel(
    total_leaves,
    levels,
    dev_ref,
    points_ref,
    charges_ref,
    basis_ref,
    ordering_ref,
    transfer_ref,
    coupling_ref,
    pay_right_ref,
    pay_left_ref,
    message_ref,
    local_ref,
    counts_ref,
    inverse_ref,
):
    device = dev_ref[0]
    rhs = charges_ref.shape[0]
    leaves = ordering_ref.shape[0]
    data_rows = pay_right_ref.shape[0] - 12 * rhs
    block = data_rows // leaves
    filler = jnp.zeros((block - rhs - 3, LANES), jnp.float32)
    for leaf in range(leaves):
        cols = slice(leaf * LANES, (leaf + 1) * LANES)
        rows = slice(leaf * block, (leaf + 1) * block)
        value = jnp.concatenate([charges_ref[:, cols], points_ref[:, cols], filler], axis=0)
        pay_right_ref[rows, :] = value
        pay_left_ref[rows, :] = value
    zero = jnp.zeros((rhs, LANES), jnp.float32)
    expansions = []
    for pair in range(leaves // 2):
        gathered = []
        for leaf in (2 * pair, 2 * pair + 1):
            ids = jnp.broadcast_to(ordering_ref[leaf : leaf + 1, :], (rhs, LANES))
            cols = slice(leaf * LANES, (leaf + 1) * LANES)
            gathered.append(jnp.take_along_axis(charges_ref[:, cols], ids, axis=1))
        left = jnp.concatenate(
            [
                jnp.concatenate([gathered[0], zero], axis=1),
                jnp.concatenate([zero, gathered[1]], axis=1),
            ],
            axis=0,
        )
        part = basis_ref[:, 2 * pair * LANES : (2 * pair + 2) * LANES]
        both = dot_t(left, jnp.concatenate([part, part], axis=0))
        expansions.append(both.reshape(2, rhs, LANES))
    current = jnp.concatenate(expansions, axis=0)
    matrix = up_matrix(transfer_ref)
    base = 0
    edge = data_rows
    for level in range(4):
        count = leaves >> level
        local_ref[base : base + count * rhs, :] = current.reshape(count * rhs, LANES)
        pay_right_ref[edge : edge + 3 * rhs, :] = current[count - 3 :].reshape(3 * rhs, LANES)
        pay_left_ref[edge : edge + 3 * rhs, :] = current[:3].reshape(3 * rhs, LANES)
        base += count * rhs
        edge += 3 * rhs
        current = up(current, matrix)
    message = packed(current[0], current[1])
    for peer in range(message_ref.shape[0] // rhs):
        message_ref[peer * rhs : (peer + 1) * rhs, :] = message
    lane = lax.broadcasted_iota(jnp.int32, (1, LANES), 1)
    starts = level_starts(total_leaves, levels)
    last = starts[-1] // LANES * LANES
    width = coupling_ref.shape[1] - last
    for level in range(levels):
        clusters = total_leaves >> level
        if starts[level] >= last:
            ids = jnp.concatenate(
                [
                    coupling_ref[:, last : last + width],
                    jnp.zeros((coupling_ref.shape[0], LANES - width), jnp.int32),
                ],
                axis=1,
            )
            targets = lane + (last - starts[level])
        else:
            count = leaves >> level if level < 4 else 2 * GROUP >> (level - 4)
            unit = device if level < 4 else device // GROUP
            tile = unit * count // LANES
            ids = coupling_ref[
                :, pl.ds(pl.multiple_of(starts[level] + tile * LANES, LANES), LANES)
            ]
            targets = lane + tile * LANES
        relative = (ids - targets) & (clusters - 1)
        for slot, shift_by in enumerate(OFFSETS):
            hits = jnp.where(relative == (shift_by & (clusters - 1)), 0.5**level, 0.0)
            counts_ref[4 * level + slot : 4 * level + slot + 1, :] = jnp.sum(
                hits, axis=0, keepdims=True
            )
    slots = lax.broadcasted_iota(jnp.int32, (LANES, LANES), 0)
    numbers = lax.broadcasted_iota(jnp.int32, (8, LANES), 1).astype(jnp.float32)
    numbers = numbers.astype(jnp.bfloat16)
    for leaf in range(leaves):
        hit = jnp.where(ordering_ref[leaf : leaf + 1, :] == slots, 1.0, 0.0).astype(jnp.bfloat16)
        found = lax.dot_general(
            numbers, hit, (((1,), (1,)), ((), ())), preferred_element_type=jnp.float32
        )
        inverse_ref[leaf : leaf + 1, :] = found[0:1].astype(jnp.int32)


def near_kernel(
    total_leaves,
    first,
    dev_ref,
    near_ref,
    own_ref,
    before_ref,
    after_ref,
    *rest,
):
    out_ref, places, weights = rest[-3:]
    rhs = out_ref.shape[0]
    leaves = near_ref.shape[1]
    entries = near_ref.shape[0]
    targets = out_ref.shape[1] // LANES
    block = (own_ref.shape[0] - 12 * rhs) // leaves
    for part, ref in enumerate((before_ref, own_ref, after_ref)):

        def fill(leaf, carry, part=part, ref=ref):
            rows = pl.multiple_of(leaf * block, 8)
            charge = ref[pl.ds(rows, rhs), :] * (0.25 / math.pi)
            high = charge.astype(jnp.bfloat16)
            low = (charge - high.astype(jnp.float32)).astype(jnp.bfloat16)
            weights[part * leaves + leaf, 0:rhs, :] = high
            weights[part * leaves + leaf, rhs : 2 * rhs, :] = low
            places[part * leaves + leaf, :, :] = ref[pl.ds(rows + rhs, 8), :]
            return carry

        lax.fori_loop(0, leaves, fill, 0, unroll=4)

    device = dev_ref[0]
    half_cycle = total_leaves // 2

    def one(step, carry):
        leaf = step + first
        target = device * leaves + leaf
        columns = jnp.transpose(places[leaves + leaf, :, :])
        axes = [
            jnp.broadcast_to(columns[:, axis : axis + 1], (LANES, LANES)) for axis in range(3)
        ]
        total = jnp.zeros((LANES, 2 * rhs), jnp.float32)
        for pair in range(entries // 2):
            highs, lows, sides = [], [], []
            for entry in (2 * pair, 2 * pair + 1):
                window = (
                    (near_ref[entry, leaf] - target + half_cycle) & (total_leaves - 1)
                ) - half_cycle
                source = leaves + leaf + window
                shift = window.astype(jnp.float32) * (1.0 / leaves)
                place = places[source, :, :]
                dx = axes[0] - (place[0:1, :] + shift)
                dy = axes[1] - place[1:2, :]
                dz = axes[2] - place[2:3, :]
                value = lax.rsqrt(dx * dx + dy * dy + (dz * dz + DELTA * DELTA))
                high = value.astype(jnp.bfloat16)
                highs.append(high)
                lows.append((value - high.astype(jnp.float32)).astype(jnp.bfloat16))
                sides.append(weights[source, :, :])
            side = jnp.concatenate(sides, axis=1)
            for piece in (jnp.concatenate(highs, axis=1), jnp.concatenate(lows, axis=1)):
                total = total + lax.dot_general(
                    piece, side, (((1,), (1,)), ((), ())), preferred_element_type=jnp.float32
                )
        turned = jnp.transpose(total)
        out_ref[:, pl.ds(pl.multiple_of(step * LANES, LANES), LANES)] = (
            turned[0:rhs, :] + turned[rhs : 2 * rhs, :]
        )
        return carry

    lax.fori_loop(0, targets, one, 0)


def couple(window, count, level, lane0, counts_ref, x_ref, row0, rows):
    for t in range(count):
        parts = [
            window(t + shift_by, slot) * counts_ref[4 * level + slot, lane0 + t]
            for slot, shift_by in enumerate(OFFSETS)
        ]
        where = slice(row0 + t * rows, row0 + (t + 1) * rows)
        x_ref[where, 0:LANES] = packed(parts[0], parts[1])
        x_ref[where, LANES : 2 * LANES] = packed(parts[2], parts[3])


def local_kernel(
    dev_ref, counts_ref, local_ref, before_ref, after_ref, stack_ref, out_ref, x_ref
):
    device = dev_ref[0]
    rhs = (before_ref.shape[0] - local_ref.shape[0] // 60 * 48) // 12
    rhs = local_ref.shape[0] // 60
    edge = before_ref.shape[0] - 12 * rhs
    base = 0
    for level in range(4):
        count = 32 >> level

        def window(t, slot, count=count, base=base, edge=edge):
            if t < 0:
                return before_ref[edge + (t + 3) * rhs : edge + (t + 4) * rhs, :]
            if t >= count:
                return after_ref[edge + (t - count) * rhs : edge + (t - count + 1) * rhs, :]
            return local_ref[base + t * rhs : base + (t + 1) * rhs, :]

        lane0 = (device * count) & (LANES - 1)
        couple(window, count, level, lane0, counts_ref, x_ref, base, rhs)
        base += count * rhs
        edge += 3 * rhs
    out_ref[...] = dot(x_ref[...], stack_ref[...])


def upper_kernel(
    total_leaves,
    dev_ref,
    counts_ref,
    gathered_ref,
    transfer_ref,
    stack_ref,
    out_ref,
    x_ref,
    top_ref,
    *sparse,
):
    device = dev_ref[0]
    index = device % GROUP
    group = device // GROUP
    rhs = out_ref.shape[0] // GROUP
    groups = gathered_ref.shape[0] // rhs
    bits = [(index >> bit) & 1 for bit in range(4)]
    matrix = up_matrix(transfer_ref)
    half = LANES // 2

    path = dot(dot(transfer_ref[bits[0]], transfer_ref[bits[1]]),
               dot(transfer_ref[bits[2]], transfer_ref[bits[3]]))
    whole = dot(matrix[:, :half], twice(path))
    level9 = dot(gathered_ref[...], whole).reshape(groups, rhs, LANES)
    level10 = up(level9, matrix)
    level11 = up(level10, matrix)
    top_ref[0:groups] = level9
    top_ref[groups : groups + groups // 2] = level10
    top_ref[groups + groups // 2 : groups + groups // 2 + groups // 4] = level11

    beside = [
        gathered_ref[pl.ds(pl.multiple_of(((group + step) & (groups - 1)) * rhs, 8), rhs), :]
        for step in range(-2, 3)
    ]
    for ref in sparse:
        ref[...] = jnp.zeros(ref.shape, jnp.float32)

    def place(ref, count, position, value):
        inside = (position >= -3) & (position < count + 3)
        ref[jnp.where(inside, position + 3, count + 6)] = value

    for step in (-1, 0, 1):
        for side, value in enumerate(unpacked(beside[step + 2])):
            place(sparse[0], 2 * GROUP, step * 2 * GROUP + 2 * index + side, value)
    current = dot(jnp.concatenate(beside, axis=0), matrix)
    for level in range(5, 9):
        count = 2 * GROUP >> (level - 4)
        reach = (-1, 0, 1) if count >= 3 else (-2, -1, 0, 1, 2)
        for step in reach:
            place(
                sparse[level - 4],
                count,
                step * count + (index >> (level - 5)),
                current[(step + 2) * rhs : (step + 3) * rhs],
            )
        if level < 8:
            current = dot(current[:, :half], twice(transfer_ref[bits[level - 5]]))

    row0 = 0
    spans = []
    for level in range(4, 9):
        count = 2 * GROUP >> (level - 4)
        ref = sparse[level - 4]
        lane0 = (group * count) & (LANES - 1)
        couple(
            lambda t, slot, ref=ref: ref[t + 3], count, level, lane0, counts_ref, x_ref, row0, rhs
        )
        spans.append((row0, count))
        row0 += count * rhs
    lane_base = LANES // 2
    top_base = 0
    for level in range(9, 12):
        clusters = groups >> (level - 9)
        cluster = group >> (level - 9)
        couple(
            lambda t, slot: top_ref[top_base + ((cluster + t) & (clusters - 1))],
            1,
            level,
            lane_base + cluster,
            counts_ref,
            x_ref,
            row0,
            rhs,
        )
        spans.append((row0, 1))
        row0 += rhs
        lane_base += clusters
        top_base += clusters
    terms = dot(x_ref[...], stack_ref[...])

    def term(level):
        start, count = spans[level - 4]
        return terms[start : start + count * rhs].reshape(count, rhs, LANES)

    current = term(11)
    for level in (10, 9):
        current = term(level) + down(current, transfer_ref, (group >> (level - 9)) & 1)
    for level in (8, 7, 6, 5, 4):
        current = term(level) + down_all(current, transfer_ref)
    paired = current.reshape(GROUP, 2, rhs, LANES)
    out_ref[...] = packed(paired[:, 0], paired[:, 1]).reshape(GROUP * rhs, LANES)


def final_kernel(
    parts_ref, terms_ref, transfer_ref, basis_ref, inverse_ref, near_a_ref, near_b_ref, out_ref
):
    rhs = out_ref.shape[0]
    leaves = inverse_ref.shape[0]
    total = parts_ref[0:rhs, :]
    for sender in range(1, GROUP):
        total = total + parts_ref[sender * rhs : (sender + 1) * rhs, :]
    left, right = unpacked(total)
    current = jnp.stack([left, right])
    base = terms_ref.shape[0]
    for level in (3, 2, 1, 0):
        count = leaves >> level
        base -= count * rhs
        mine = terms_ref[base : base + count * rhs, :].reshape(count, rhs, LANES)
        current = mine + down_all(current, transfer_ref)
    lane = lax.broadcasted_iota(jnp.int32, (rhs, LANES), 1)
    low = lane < LANES // 2
    zero = jnp.zeros((rhs, LANES), jnp.float32)
    for four in range(leaves // 4):
        rows, sides = [], []
        for slot in range(4):
            leaf = 4 * four + slot
            value = jnp.where(low if slot % 2 == 0 else ~low, current[leaf], 0.0)
            rows.append(jnp.concatenate([value, zero] if slot < 2 else [zero, value], axis=1))
            sides.append(basis_ref[:, leaf * LANES : (leaf + 1) * LANES])
        far = dot(jnp.concatenate(rows, axis=0), jnp.concatenate(sides, axis=0))
        for slot in range(4):
            leaf = 4 * four + slot
            ids = jnp.broadcast_to(inverse_ref[leaf : leaf + 1, :], (rhs, LANES))
            value = jnp.take_along_axis(far[slot * rhs : (slot + 1) * rhs], ids, axis=1)
            near_ref = near_a_ref if leaf < leaves // 2 else near_b_ref
            at = leaf % (leaves // 2) * LANES
            out_ref[:, leaf * LANES : (leaf + 1) * LANES] = value + near_ref[:, at : at + LANES]


def call(kernel, outs, scalars, operands, scratch=(), cost=None):
    smem = pl.BlockSpec(memory_space=pltpu.SMEM)
    vmem = pl.BlockSpec(memory_space=pltpu.VMEM)
    return pl.pallas_call(
        kernel,
        out_shape=outs,
        in_specs=[smem] * len(scalars) + [vmem] * len(operands),
        out_specs=jax.tree.map(lambda _: vmem, outs),
        scratch_shapes=list(scratch),
        cost_estimate=cost,
        compiler_params=pltpu.CompilerParams(vmem_limit_bytes=VMEM_BYTES),
    )(*scalars, *operands)


def local(points, charges, basis, transfer, near_list, coupling_list, ordering):
    devices = lax.axis_size("leaf")
    device = jnp.reshape(lax.axis_index("leaf"), (1,)).astype(jnp.int32)
    leaves = near_list.shape[1]
    rhs = charges.shape[0]
    total_leaves = leaves * devices
    levels = total_leaves.bit_length() - 3
    groups = devices // GROUP
    f32 = jnp.float32
    ids = ordering.reshape(leaves, LANES)
    stack = jnp.asarray(coupling_stack())
    pay_rows = leaves * 24 + 12 * rhs
    local_rows = (leaves * 2 - 4) * rhs

    pay_right, pay_left, message, local_terms, counts, inverse = call(
        lambda *refs: prepare_kernel(total_leaves, levels, *refs),
        [
            jax.ShapeDtypeStruct((pay_rows, LANES), f32),
            jax.ShapeDtypeStruct((pay_rows, LANES), f32),
            jax.ShapeDtypeStruct((groups * rhs, LANES), f32),
            jax.ShapeDtypeStruct((local_rows, LANES), f32),
            jax.ShapeDtypeStruct((4 * levels, LANES), f32),
            jax.ShapeDtypeStruct((leaves, LANES), jnp.int32),
        ],
        [device],
        [points, charges, basis, ids, transfer, coupling_list],
    )
    before = lax.ppermute(pay_right, "leaf", [(i, (i + 1) % devices) for i in range(devices)])
    after = lax.ppermute(pay_left, "leaf", [((i + 1) % devices, i) for i in range(devices)])
    gathered = lax.all_to_all(
        message,
        "leaf",
        0,
        0,
        axis_index_groups=[[g * GROUP + i for g in range(groups)] for i in range(GROUP)],
        tiled=True,
    )

    def near(first, count, extra):
        return call(
            lambda *refs: near_kernel(total_leaves, first, *refs),
            jax.ShapeDtypeStruct((rhs, count * LANES), f32),
            [device, near_list],
            [pay_right, before, after, *extra],
            [
                pltpu.VMEM((3 * leaves, 8, LANES), f32),
                pltpu.VMEM((3 * leaves, 2 * rhs, LANES), jnp.bfloat16),
            ],
            pl.CostEstimate(
                flops=count * 12 * 128 * 128 * 100,
                bytes_accessed=8 << 20,
                transcendentals=count * 12 * 128 * 128,
            ),
        )

    near_a = near(0, leaves // 2, [])
    terms = call(
        local_kernel,
        jax.ShapeDtypeStruct((local_rows, LANES), f32),
        [device, counts],
        [local_terms, before, after, stack],
        [pltpu.VMEM((local_rows, 2 * LANES), f32)],
    )
    upper_rows = (4 * GROUP - 2 + 3) * rhs
    spread = call(
        lambda *refs: upper_kernel(total_leaves, *refs),
        jax.ShapeDtypeStruct((GROUP * rhs, LANES), f32),
        [device, counts],
        [gathered, transfer, stack],
        [
            pltpu.VMEM((upper_rows, 2 * LANES), f32),
            pltpu.VMEM((2 * groups, rhs, LANES), f32),
            *[
                pltpu.VMEM(((2 * GROUP >> step) + 7, rhs, LANES), f32)
                for step in range(5)
            ],
        ],
    )
    parts = lax.all_to_all(
        spread,
        "leaf",
        0,
        0,
        axis_index_groups=[[g * GROUP + i for i in range(GROUP)] for g in range(groups)],
        tiled=True,
    )
    near_b = near(leaves // 2, leaves // 2, [spread])
    return call(
        final_kernel,
        jax.ShapeDtypeStruct(charges.shape, f32),
        [],
        [parts, terms, transfer, basis, inverse, near_a, near_b],
    )


def solution(mesh):
    placed = (
        P(None, "leaf"),
        P(None, "leaf"),
        P(None, "leaf"),
        P(),
        P(None, "leaf"),
        P(),
        P("leaf"),
    )
    return jax.shard_map(
        local, mesh=mesh, in_specs=placed, out_specs=P(None, "leaf"), check_vma=False
    )
```

```python
import math

import jax
import jax.numpy as jnp
import numpy as np
from jax import lax
from jax.experimental import pallas as pl
from jax.experimental.pallas import tpu as pltpu
from jax.sharding import PartitionSpec as P

ORDER = 4
OFFSETS = (2, 3, -3, -2)
DELTA = 0.05
PROXY = 0.35
GROUP = 16
LANES = 128
VMEM_BYTES = 50 * 1024 * 1024
FIRST_BYTES = 61 * 1024 * 1024


def coupling_stack():
    nodes = np.cos((2.0 * np.arange(ORDER) + 1.0) * (math.pi / (2.0 * ORDER)))
    grid = np.stack(np.meshgrid(nodes, nodes, nodes, indexing="ij")).reshape(3, -1) * PROXY
    stacked = []
    for shift_by in OFFSETS:
        moved = grid + np.array([float(shift_by), 0.0, 0.0])[:, None]
        difference = grid[:, :, None] - moved[:, None, :]
        stacked.append((0.25 / math.pi / np.sqrt((difference**2).sum(0))).T)
    table = np.concatenate(stacked, axis=0)
    return np.concatenate([table, table], axis=1).astype(np.float32)


def halves(value):
    high = value.astype(jnp.bfloat16)
    return high, (value - high.astype(jnp.float32)).astype(jnp.bfloat16)


def bf16_dot(left, right, dims):
    return lax.dot_general(left, right, (dims, ((), ())), preferred_element_type=jnp.float32)


def summed(product, rows, columns):
    return product[:rows, :columns] + (product[:rows, columns:] + product[rows:, :columns])


def dot(left, right):
    both = bf16_dot(
        jnp.concatenate(halves(left), axis=0), jnp.concatenate(halves(right), axis=1), ((1,), (0,))
    )
    return summed(both, left.shape[0], right.shape[1])


def dot_t(left, right):
    both = bf16_dot(
        jnp.concatenate(halves(left), axis=0), jnp.concatenate(halves(right), axis=0), ((1,), (1,))
    )
    return summed(both, left.shape[0], right.shape[0])


def first_half(shape):
    return lax.broadcasted_iota(jnp.int32, shape, len(shape) - 1) < LANES // 2


def packed(left, right):
    return jnp.where(first_half(left.shape), left, right)


def unpacked(both):
    turned = pltpu.roll(both, LANES // 2, 1)
    return packed(both, turned), packed(turned, both)


def twice(matrix):
    return jnp.concatenate([matrix, matrix], axis=1)


def up_matrix(transfer_ref):
    return jnp.concatenate([twice(transfer_ref[0]), twice(transfer_ref[1])], axis=0)


def up(values, matrix):
    count, rows, lanes = values.shape
    both = paired(values).reshape(count // 2 * rows, lanes)
    return dot(both, matrix).reshape(count // 2, rows, lanes)


def down(parent, matrix):
    doubled = jnp.concatenate([matrix, matrix], axis=0)
    return dot_t(parent[:, : LANES // 2], doubled)


def down_matrix(transfer_ref):
    both = jnp.concatenate([transfer_ref[0], transfer_ref[1]], axis=0)
    zero = jnp.zeros(both.shape, jnp.float32)
    return jnp.concatenate(
        [jnp.concatenate([both, zero], axis=1), jnp.concatenate([zero, both], axis=1)], axis=0
    )


def down_pairs(pairs, matrix):
    count, rows, lanes = pairs.shape
    both = dot_t(pairs.reshape(count * rows, lanes), matrix).reshape(count, rows, 2 * lanes)
    return jnp.stack([both[:, :, :lanes], both[:, :, lanes:]], axis=1).reshape(
        2 * count, rows, lanes
    )


def paired(values):
    count, rows, lanes = values.shape
    pairs = values.reshape(count // 2, 2, rows, lanes)
    return packed(pairs[:, 0], pairs[:, 1])


def level_starts(total_leaves, levels):
    return [2 * total_leaves - 2 * (total_leaves >> level) for level in range(levels)]


def prepare_kernel(
    total_leaves,
    levels,
    dev_ref,
    points_in,
    charges_in,
    basis_in,
    ordering_in,
    transfer_in,
    coupling_in,
    pay_right_ref,
    pay_left_ref,
    message_ref,
    local_ref,
    counts_ref,
    inverse_ref,
    points_ref,
    charges_ref,
    basis_ref,
    ordering_ref,
    transfer_ref,
    coupling_ref,
    arrived,
):
    device = dev_ref[0]
    moves = [
        (charges_in, charges_ref),
        (ordering_in, ordering_ref),
        (points_in, points_ref),
        (transfer_in, transfer_ref),
    ]
    quarter = basis_in.shape[1] // 4
    for part in range(4):
        cols = pl.ds(part * quarter, quarter)
        moves.append((basis_in.at[:, cols], basis_ref.at[:, cols]))
    moves.append((coupling_in, coupling_ref))
    copies = [
        pltpu.make_async_copy(source, target, arrived.at[slot])
        for slot, (source, target) in enumerate(moves)
    ]
    for copy in copies:
        copy.start()
    for copy in copies[:3]:
        copy.wait()
    rhs = charges_ref.shape[0]
    leaves = ordering_ref.shape[0]
    data_rows = pay_right_ref.shape[0] - 12 * rhs
    block = data_rows // leaves
    filler = jnp.zeros((block - rhs - 3, LANES), jnp.float32)
    for leaf in range(leaves):
        cols = slice(leaf * LANES, (leaf + 1) * LANES)
        rows = slice(leaf * block, (leaf + 1) * block)
        value = jnp.concatenate([charges_ref[:, cols], points_ref[:, cols], filler], axis=0)
        pay_right_ref[rows, :] = value
        pay_left_ref[rows, :] = value
    zero = jnp.zeros((rhs, LANES), jnp.float32)
    expansions = []
    for pair in range(leaves // 2):
        if pair % (leaves // 8) == 0:
            copies[4 + pair // (leaves // 8)].wait()
        gathered = []
        for leaf in (2 * pair, 2 * pair + 1):
            ids = jnp.broadcast_to(ordering_ref[leaf : leaf + 1, :], (rhs, LANES))
            cols = slice(leaf * LANES, (leaf + 1) * LANES)
            gathered.append(jnp.take_along_axis(charges_ref[:, cols], ids, axis=1))
        left = jnp.concatenate(
            [
                jnp.concatenate([gathered[0], zero], axis=1),
                jnp.concatenate([zero, gathered[1]], axis=1),
            ],
            axis=0,
        )
        part = basis_ref[:, 2 * pair * LANES : (2 * pair + 2) * LANES]
        both = dot_t(left, jnp.concatenate([part, part], axis=0))
        expansions.append(both.reshape(2, rhs, LANES))
    current = jnp.concatenate(expansions, axis=0)
    copies[3].wait()
    matrix = up_matrix(transfer_ref)
    base = 0
    edge = data_rows
    for level in range(4):
        count = leaves >> level
        local_ref[base : base + count * rhs, :] = current.reshape(count * rhs, LANES)
        pay_right_ref[edge : edge + 3 * rhs, :] = current[count - 3 :].reshape(3 * rhs, LANES)
        pay_left_ref[edge : edge + 3 * rhs, :] = current[:3].reshape(3 * rhs, LANES)
        base += count * rhs
        edge += 3 * rhs
        current = up(current, matrix)
    message = packed(current[0], current[1])
    for peer in range(message_ref.shape[0] // rhs):
        message_ref[peer * rhs : (peer + 1) * rhs, :] = message
    copies[8].wait()
    lane = lax.broadcasted_iota(jnp.int32, (1, LANES), 1)
    starts = level_starts(total_leaves, levels)
    last = starts[-1] // LANES * LANES
    width = coupling_ref.shape[1] - last
    for level in range(levels):
        clusters = total_leaves >> level
        if starts[level] >= last:
            ids = jnp.concatenate(
                [
                    coupling_ref[:, last : last + width],
                    jnp.zeros((coupling_ref.shape[0], LANES - width), jnp.int32),
                ],
                axis=1,
            )
            targets = lane + (last - starts[level])
        else:
            count = leaves >> level if level < 4 else 2 * GROUP >> (level - 4)
            unit = device if level < 4 else device // GROUP
            tile = unit * count // LANES
            ids = coupling_ref[
                :, pl.ds(pl.multiple_of(starts[level] + tile * LANES, LANES), LANES)
            ]
            targets = lane + tile * LANES
        relative = (ids - targets) & (clusters - 1)
        for slot, shift_by in enumerate(OFFSETS):
            hits = jnp.where(relative == (shift_by & (clusters - 1)), 0.5**level, 0.0)
            counts_ref[4 * level + slot : 4 * level + slot + 1, :] = jnp.sum(
                hits, axis=0, keepdims=True
            )
    slots = lax.broadcasted_iota(jnp.int32, (LANES, LANES), 0)
    numbers = lax.broadcasted_iota(jnp.int32, (8, LANES), 1).astype(jnp.float32)
    numbers = numbers.astype(jnp.bfloat16)
    for leaf in range(leaves):
        hit = jnp.where(ordering_ref[leaf : leaf + 1, :] == slots, 1.0, 0.0).astype(jnp.bfloat16)
        found = lax.dot_general(
            numbers, hit, (((1,), (1,)), ((), ())), preferred_element_type=jnp.float32
        )
        inverse_ref[leaf : leaf + 1, :] = found[0:1].astype(jnp.int32)


def near_kernel(
    total_leaves,
    first,
    dev_ref,
    near_ref,
    own_ref,
    before_ref,
    after_ref,
    *rest,
):
    out_ref, places, weights = rest[-3:]
    rhs = out_ref.shape[0]
    leaves = near_ref.shape[1]
    entries = near_ref.shape[0]
    targets = out_ref.shape[1] // LANES
    block = (own_ref.shape[0] - 12 * rhs) // leaves
    for part, ref in enumerate((before_ref, own_ref, after_ref)):

        def fill(leaf, carry, part=part, ref=ref):
            rows = pl.multiple_of(leaf * block, 8)
            charge = ref[pl.ds(rows, rhs), :] * (0.25 / math.pi)
            high = charge.astype(jnp.bfloat16)
            low = (charge - high.astype(jnp.float32)).astype(jnp.bfloat16)
            weights[part * leaves + leaf, 0:rhs, :] = high
            weights[part * leaves + leaf, rhs : 2 * rhs, :] = low
            places[part * leaves + leaf, :, :] = ref[pl.ds(rows + rhs, 8), :]
            return carry

        lax.fori_loop(0, leaves, fill, 0, unroll=4)

    device = dev_ref[0]
    half_cycle = total_leaves // 2

    def one(step, carry):
        leaf = step + first
        target = device * leaves + leaf
        columns = jnp.transpose(places[leaves + leaf, :, :])
        axes = [
            jnp.broadcast_to(columns[:, axis : axis + 1], (LANES, LANES)) for axis in range(3)
        ]
        total = jnp.zeros((2 * rhs, LANES), jnp.float32)
        for pair in range(entries // 2):
            highs, lows, sides = [], [], []
            for entry in (2 * pair, 2 * pair + 1):
                window = (
                    (near_ref[entry, leaf] - target + half_cycle) & (total_leaves - 1)
                ) - half_cycle
                source = leaves + leaf + window
                shift = window.astype(jnp.float32) * (1.0 / leaves)
                place = places[source, :, :]
                dx = axes[0] - (place[0:1, :] + shift)
                dy = axes[1] - place[1:2, :]
                dz = axes[2] - place[2:3, :]
                value = lax.rsqrt(dx * dx + dy * dy + (dz * dz + DELTA * DELTA))
                high = value.astype(jnp.bfloat16)
                highs.append(high)
                lows.append((value - high.astype(jnp.float32)).astype(jnp.bfloat16))
                sides.append(weights[source, :, :])
            side = jnp.concatenate(sides, axis=1)
            for piece in (jnp.concatenate(highs, axis=1), jnp.concatenate(lows, axis=1)):
                total = total + bf16_dot(side, piece, ((1,), (1,)))
        out_ref[:, pl.ds(pl.multiple_of(step * LANES, LANES), LANES)] = (
            total[0:rhs, :] + total[rhs : 2 * rhs, :]
        )
        return carry

    lax.fori_loop(0, targets, one, 0, unroll=4)


def couple(window, count, level, lane0, counts_ref, x_ref, row0, rows):
    for t in range(count):
        parts = [
            window(t + shift_by, slot) * counts_ref[4 * level + slot, lane0 + t]
            for slot, shift_by in enumerate(OFFSETS)
        ]
        where = slice(row0 + t * rows, row0 + (t + 1) * rows)
        x_ref[where, 0:LANES] = packed(parts[0], parts[1])
        x_ref[where, LANES : 2 * LANES] = packed(parts[2], parts[3])


def local_kernel(
    dev_ref, counts_ref, local_ref, before_ref, after_ref, stack_ref, out_ref, x_ref
):
    device = dev_ref[0]
    rhs = local_ref.shape[0] // 60
    edge = before_ref.shape[0] - 12 * rhs
    base = 0
    for level in range(4):
        count = 32 >> level

        def window(t, slot, count=count, base=base, edge=edge):
            if t < 0:
                return before_ref[edge + (t + 3) * rhs : edge + (t + 4) * rhs, :]
            if t >= count:
                return after_ref[edge + (t - count) * rhs : edge + (t - count + 1) * rhs, :]
            return local_ref[base + t * rhs : base + (t + 1) * rhs, :]

        lane0 = (device * count) & (LANES - 1)
        couple(window, count, level, lane0, counts_ref, x_ref, base, rhs)
        base += count * rhs
        edge += 3 * rhs
    terms = dot(x_ref[...], stack_ref[...])
    pairs = paired(terms.reshape(-1, rhs, LANES))
    out_ref[...] = pairs.reshape(out_ref.shape)


def upper_kernel(
    total_leaves,
    dev_ref,
    counts_ref,
    gathered_ref,
    transfer_ref,
    stack_ref,
    _,
    out_ref,
    x_ref,
    top_ref,
    *sparse,
):
    device = dev_ref[0]
    index = device % GROUP
    group = device // GROUP
    rhs = out_ref.shape[0] // GROUP
    groups = gathered_ref.shape[0] // rhs
    bits = [(index >> bit) & 1 for bit in range(4)]
    matrix = up_matrix(transfer_ref)
    half = LANES // 2

    path = dot(dot(transfer_ref[bits[0]], transfer_ref[bits[1]]),
               dot(transfer_ref[bits[2]], transfer_ref[bits[3]]))
    whole = dot(matrix[:, :half], twice(path))
    level9 = dot(gathered_ref[...], whole).reshape(groups, rhs, LANES)
    level10 = up(level9, matrix)
    level11 = up(level10, matrix)
    top_ref[0:groups] = level9
    top_ref[groups : groups + groups // 2] = level10
    top_ref[groups + groups // 2 : groups + groups // 2 + groups // 4] = level11

    beside = [
        gathered_ref[pl.ds(pl.multiple_of(((group + step) & (groups - 1)) * rhs, 8), rhs), :]
        for step in range(-2, 3)
    ]
    for ref in sparse:
        ref[...] = jnp.zeros(ref.shape, jnp.float32)

    def place(ref, count, position, value):
        inside = (position >= -3) & (position < count + 3)
        ref[jnp.where(inside, position + 3, count + 6)] = value

    for step in (-1, 0, 1):
        for side, value in enumerate(unpacked(beside[step + 2])):
            place(sparse[0], 2 * GROUP, step * 2 * GROUP + 2 * index + side, value)
    current = dot(jnp.concatenate(beside, axis=0), matrix)
    for level in range(5, 9):
        count = 2 * GROUP >> (level - 4)
        reach = (-1, 0, 1) if count >= 3 else (-2, -1, 0, 1, 2)
        for step in reach:
            place(
                sparse[level - 4],
                count,
                step * count + (index >> (level - 5)),
                current[(step + 2) * rhs : (step + 3) * rhs],
            )
        if level < 8:
            current = dot(current[:, :half], twice(transfer_ref[bits[level - 5]]))

    row0 = 0
    spans = []
    for level in range(4, 9):
        count = 2 * GROUP >> (level - 4)
        ref = sparse[level - 4]
        lane0 = (group * count) & (LANES - 1)
        couple(
            lambda t, slot, ref=ref: ref[t + 3], count, level, lane0, counts_ref, x_ref, row0, rhs
        )
        spans.append((row0, count))
        row0 += count * rhs
    lane_base = LANES // 2
    top_base = 0
    for level in range(9, 12):
        clusters = groups >> (level - 9)
        cluster = group >> (level - 9)
        couple(
            lambda t, slot: top_ref[top_base + ((cluster + t) & (clusters - 1))],
            1,
            level,
            lane_base + cluster,
            counts_ref,
            x_ref,
            row0,
            rhs,
        )
        spans.append((row0, 1))
        row0 += rhs
        lane_base += clusters
        top_base += clusters
    terms = dot(x_ref[...], stack_ref[...])

    def term(level):
        start, count = spans[level - 4]
        return terms[start : start + count * rhs].reshape(count, rhs, LANES)

    current = term(11)[0]
    for level in (10, 9):
        child = (group >> (level - 9)) & 1
        current = term(level)[0] + down(current, transfer_ref[child])
    both = jnp.concatenate([transfer_ref[0], transfer_ref[1]], axis=0)
    current = (dot_t(current[:, :half], both) + paired(term(8))[0])[None]
    matrix = down_matrix(transfer_ref)
    for level in (7, 6, 5, 4):
        current = paired(term(level)) + down_pairs(current, matrix)
    out_ref[...] = current.reshape(out_ref.shape)


def final_kernel(
    parts_ref, terms_ref, transfer_ref, basis_ref, inverse_ref, near_a_ref, near_b_ref, out_ref
):
    rhs = out_ref.shape[0]
    leaves = inverse_ref.shape[0]
    total = parts_ref[0:rhs, :]
    for sender in range(1, GROUP):
        total = total + parts_ref[sender * rhs : (sender + 1) * rhs, :]
    current = total[None]
    matrix = down_matrix(transfer_ref)
    base = terms_ref.shape[0]
    for level in (3, 2, 1, 0):
        count = leaves >> level + 1
        base -= count * rhs
        mine = terms_ref[base : base + count * rhs, :].reshape(count, rhs, LANES)
        current = mine + down_pairs(current, matrix)
    lane = lax.broadcasted_iota(jnp.int32, (rhs, LANES), 1)
    low = lane < LANES // 2
    zero = jnp.zeros((rhs, LANES), jnp.float32)
    for four in range(leaves // 4):
        rows, sides = [], []
        for slot in range(4):
            leaf = 4 * four + slot
            value = jnp.where(low if slot % 2 == 0 else ~low, current[leaf // 2], 0.0)
            rows.append(jnp.concatenate([value, zero] if slot < 2 else [zero, value], axis=1))
            sides.append(basis_ref[:, leaf * LANES : (leaf + 1) * LANES])
        far = dot(jnp.concatenate(rows, axis=0), jnp.concatenate(sides, axis=0))
        for slot in range(4):
            leaf = 4 * four + slot
            ids = jnp.broadcast_to(inverse_ref[leaf : leaf + 1, :], (rhs, LANES))
            value = jnp.take_along_axis(far[slot * rhs : (slot + 1) * rhs], ids, axis=1)
            near_ref = near_a_ref if leaf < leaves // 2 else near_b_ref
            at = leaf % (leaves // 2) * LANES
            out_ref[:, leaf * LANES : (leaf + 1) * LANES] = value + near_ref[:, at : at + LANES]


def call(kernel, outs, scalars, operands, scratch=(), cost=None, kept=(), limit=VMEM_BYTES):
    smem = pl.BlockSpec(memory_space=pltpu.SMEM)
    vmem = pl.BlockSpec(memory_space=pltpu.VMEM)
    hbm = pl.BlockSpec(memory_space=pltpu.HBM)
    return pl.pallas_call(
        kernel,
        out_shape=outs,
        in_specs=[smem] * len(scalars) + [vmem] * len(operands) + [hbm] * len(kept),
        out_specs=jax.tree.map(lambda _: vmem, outs),
        scratch_shapes=list(scratch),
        cost_estimate=cost,
        compiler_params=pltpu.CompilerParams(vmem_limit_bytes=limit),
    )(*scalars, *operands, *kept)


def local(points, charges, basis, transfer, near_list, coupling_list, ordering):
    devices = lax.axis_size("leaf")
    device = jnp.reshape(lax.axis_index("leaf"), (1,)).astype(jnp.int32)
    leaves = near_list.shape[1]
    rhs = charges.shape[0]
    total_leaves = leaves * devices
    levels = total_leaves.bit_length() - 3
    groups = devices // GROUP
    f32 = jnp.float32
    ids = ordering.reshape(leaves, LANES)
    stack = jnp.asarray(coupling_stack())
    pay_rows = leaves * 24 + 12 * rhs
    local_rows = (leaves * 2 - 4) * rhs

    inputs = [points, charges, basis, ids, transfer, coupling_list]
    pay_right, pay_left, message, local_terms, counts, inverse = call(
        lambda *refs: prepare_kernel(total_leaves, levels, *refs),
        [
            jax.ShapeDtypeStruct((pay_rows, LANES), f32),
            jax.ShapeDtypeStruct((pay_rows, LANES), f32),
            jax.ShapeDtypeStruct((groups * rhs, LANES), f32),
            jax.ShapeDtypeStruct((local_rows, LANES), f32),
            jax.ShapeDtypeStruct((4 * levels, LANES), f32),
            jax.ShapeDtypeStruct((leaves, LANES), jnp.int32),
        ],
        [device],
        [],
        [
            *[pltpu.VMEM(array.shape, array.dtype) for array in inputs],
            pltpu.SemaphoreType.DMA((len(inputs) + 3,)),
        ],
        kept=inputs,
        limit=FIRST_BYTES,
    )
    before = lax.ppermute(pay_right, "leaf", [(i, (i + 1) % devices) for i in range(devices)])
    after = lax.ppermute(pay_left, "leaf", [((i + 1) % devices, i) for i in range(devices)])
    gathered = lax.all_to_all(
        message,
        "leaf",
        0,
        0,
        axis_index_groups=[[g * GROUP + i for g in range(groups)] for i in range(GROUP)],
        tiled=True,
    )

    def near(first, count, extra):
        return call(
            lambda *refs: near_kernel(total_leaves, first, *refs),
            jax.ShapeDtypeStruct((rhs, count * LANES), f32),
            [device, near_list],
            [pay_right, before, after],
            [
                pltpu.VMEM((3 * leaves, 8, LANES), f32),
                pltpu.VMEM((3 * leaves, 2 * rhs, LANES), jnp.bfloat16),
            ],
            pl.CostEstimate(
                flops=count * 12 * 128 * 128 * 100,
                bytes_accessed=8 << 20,
                transcendentals=count * 12 * 128 * 128,
            ),
            kept=extra,
        )

    near_a = near(0, leaves // 2, [])
    terms = call(
        local_kernel,
        jax.ShapeDtypeStruct((local_rows // 2, LANES), f32),
        [device, counts],
        [local_terms, before, after, stack],
        [pltpu.VMEM((local_rows, 2 * LANES), f32)],
    )
    upper_rows = (4 * GROUP - 2 + 3) * rhs
    spread = call(
        lambda *refs: upper_kernel(total_leaves, *refs),
        jax.ShapeDtypeStruct((GROUP * rhs, LANES), f32),
        [device, counts],
        [gathered, transfer, stack],
        [
            pltpu.VMEM((upper_rows, 2 * LANES), f32),
            pltpu.VMEM((2 * groups, rhs, LANES), f32),
            *[
                pltpu.VMEM(((2 * GROUP >> step) + 7, rhs, LANES), f32)
                for step in range(5)
            ],
        ],
        kept=[near_a],
    )
    parts = lax.all_to_all(
        spread,
        "leaf",
        0,
        0,
        axis_index_groups=[[g * GROUP + i for i in range(GROUP)] for g in range(groups)],
        tiled=True,
    )
    near_b = near(leaves // 2, leaves // 2, [spread])
    return call(
        final_kernel,
        jax.ShapeDtypeStruct(charges.shape, f32),
        [],
        [parts, terms, transfer, basis, inverse, near_a, near_b],
    )


def solution(mesh):
    placed = (
        P(None, "leaf"),
        P(None, "leaf"),
        P(None, "leaf"),
        P(),
        P(None, "leaf"),
        P(),
        P("leaf"),
    )
    return jax.shard_map(
        local, mesh=mesh, in_specs=placed, out_specs=P(None, "leaf"), check_vma=False
    )
```

```python
import math

import jax
import jax.numpy as jnp
import numpy as np
from jax import lax
from jax.experimental import pallas as pl
from jax.experimental.pallas import tpu as pltpu
from jax.sharding import PartitionSpec as P

ORDER = 4
OFFSETS = (2, 3, -3, -2)
DELTA = 0.05
PROXY = 0.35
GROUP = 16
LANES = 128
VMEM_BYTES = 50 * 1024 * 1024
FIRST_BYTES = 61 * 1024 * 1024


def coupling_stack():
    nodes = np.cos((2.0 * np.arange(ORDER) + 1.0) * (math.pi / (2.0 * ORDER)))
    grid = np.stack(np.meshgrid(nodes, nodes, nodes, indexing="ij")).reshape(3, -1) * PROXY
    stacked = []
    for shift_by in OFFSETS:
        moved = grid + np.array([float(shift_by), 0.0, 0.0])[:, None]
        difference = grid[:, :, None] - moved[:, None, :]
        stacked.append((0.25 / math.pi / np.sqrt((difference**2).sum(0))).T)
    table = np.concatenate(stacked, axis=0)
    return np.concatenate([table, table], axis=1).astype(np.float32)


def halves(value):
    high = value.astype(jnp.bfloat16)
    return high, (value - high.astype(jnp.float32)).astype(jnp.bfloat16)


def bf16_dot(left, right, dims):
    return lax.dot_general(left, right, (dims, ((), ())), preferred_element_type=jnp.float32)


def summed(product, rows, columns):
    return product[:rows, :columns] + (product[:rows, columns:] + product[rows:, :columns])


def dot(left, right):
    both = bf16_dot(
        jnp.concatenate(halves(left), axis=0), jnp.concatenate(halves(right), axis=1), ((1,), (0,))
    )
    return summed(both, left.shape[0], right.shape[1])


def dot_t(left, right):
    both = bf16_dot(
        jnp.concatenate(halves(left), axis=0), jnp.concatenate(halves(right), axis=0), ((1,), (1,))
    )
    return summed(both, left.shape[0], right.shape[0])


def first_half(shape):
    return lax.broadcasted_iota(jnp.int32, shape, len(shape) - 1) < LANES // 2


def packed(left, right):
    return jnp.where(first_half(left.shape), left, right)


def unpacked(both):
    turned = pltpu.roll(both, LANES // 2, 1)
    return packed(both, turned), packed(turned, both)


def twice(matrix):
    return jnp.concatenate([matrix, matrix], axis=1)


def up_matrix(transfer_ref):
    return jnp.concatenate([twice(transfer_ref[0]), twice(transfer_ref[1])], axis=0)


def up(values, matrix):
    count, rows, lanes = values.shape
    both = paired(values).reshape(count // 2 * rows, lanes)
    return dot(both, matrix).reshape(count // 2, rows, lanes)


def down(parent, matrix):
    doubled = jnp.concatenate([matrix, matrix], axis=0)
    return dot_t(parent[:, : LANES // 2], doubled)


def down_matrix(transfer_ref):
    both = jnp.concatenate([transfer_ref[0], transfer_ref[1]], axis=0)
    zero = jnp.zeros(both.shape, jnp.float32)
    return jnp.concatenate(
        [jnp.concatenate([both, zero], axis=1), jnp.concatenate([zero, both], axis=1)], axis=0
    )


def down_pairs(pairs, matrix):
    count, rows, lanes = pairs.shape
    both = dot_t(pairs.reshape(count * rows, lanes), matrix).reshape(count, rows, 2 * lanes)
    return jnp.stack([both[:, :, :lanes], both[:, :, lanes:]], axis=1).reshape(
        2 * count, rows, lanes
    )


def paired(values):
    count, rows, lanes = values.shape
    pairs = values.reshape(count // 2, 2, rows, lanes)
    return packed(pairs[:, 0], pairs[:, 1])


def level_starts(total_leaves, levels):
    return [2 * total_leaves - 2 * (total_leaves >> level) for level in range(levels)]


def prepare_kernel(
    total_leaves,
    levels,
    dev_ref,
    points_in,
    charges_in,
    basis_in,
    ordering_in,
    transfer_in,
    coupling_in,
    pay_right_ref,
    pay_left_ref,
    message_ref,
    local_ref,
    counts_ref,
    inverse_ref,
    paths_ref,
    points_ref,
    charges_ref,
    basis_ref,
    ordering_ref,
    transfer_ref,
    coupling_ref,
    data_ref,
    edge_ref,
    arrived,
):
    device = dev_ref[0]
    moves = [
        (charges_in, charges_ref),
        (points_in, points_ref),
        (ordering_in, ordering_ref),
        (transfer_in, transfer_ref),
        (basis_in, basis_ref),
        (coupling_in, coupling_ref),
    ]
    copies = [
        pltpu.make_async_copy(source, target, arrived.at[slot])
        for slot, (source, target) in enumerate(moves)
    ]
    for copy in copies:
        copy.start()
    rhs = charges_ref.shape[0]
    leaves = ordering_ref.shape[0]
    data_rows = leaves * (rhs + 3)
    copies[0].wait()
    copies[1].wait()
    for leaf in range(leaves):
        cols = slice(leaf * LANES, (leaf + 1) * LANES)
        data_ref[leaf * rhs : (leaf + 1) * rhs, :] = charges_ref[:, cols]
        for axis in range(3):
            at = leaves * (rhs + axis) + leaf
            data_ref[at : at + 1, :] = points_ref[axis : axis + 1, cols]
    sent = [
        pltpu.make_async_copy(
            data_ref, target.at[pl.ds(0, data_rows), :], arrived.at[len(moves) + slot]
        )
        for slot, target in enumerate((pay_right_ref, pay_left_ref))
    ]
    for copy in sent:
        copy.start()
    copies[2].wait()
    slots = lax.broadcasted_iota(jnp.int32, (LANES, LANES), 0)
    numbers = lax.broadcasted_iota(jnp.int32, (16, LANES), 1).astype(jnp.float32)
    numbers = numbers.astype(jnp.bfloat16)
    for leaf in range(leaves):
        hit = jnp.where(ordering_ref[leaf : leaf + 1, :] == slots, 1.0, 0.0).astype(jnp.bfloat16)
        found = bf16_dot(numbers, hit, ((1,), (1,)))
        inverse_ref[leaf : leaf + 1, :] = found[0:1].astype(jnp.int32)
    zero = jnp.zeros((rhs, LANES), jnp.float32)
    expansions = []
    for copy in copies[3:]:
        copy.wait()
    for pair in range(leaves // 2):
        gathered = []
        for leaf in (2 * pair, 2 * pair + 1):
            ids = jnp.broadcast_to(ordering_ref[leaf : leaf + 1, :], (rhs, LANES))
            cols = slice(leaf * LANES, (leaf + 1) * LANES)
            gathered.append(jnp.take_along_axis(charges_ref[:, cols], ids, axis=1))
        left = jnp.concatenate(
            [
                jnp.concatenate([gathered[0], zero], axis=1),
                jnp.concatenate([zero, gathered[1]], axis=1),
            ],
            axis=0,
        )
        part = basis_ref[:, 2 * pair * LANES : (2 * pair + 2) * LANES]
        both = dot_t(left, jnp.concatenate([part, part], axis=0))
        expansions.append(both.reshape(2, rhs, LANES))
    current = jnp.concatenate(expansions, axis=0)
    matrix = up_matrix(transfer_ref)
    path = matrix
    for level in range(5, 10):
        paths_ref[:, (level - 5) * LANES : (level - 4) * LANES] = path
        if level < 9:
            bit = ((device % GROUP) >> (level - 5)) & 1
            path = dot(path[:, : LANES // 2], twice(transfer_ref[bit]))
    base = 0
    lasts, firsts = [], []
    for level in range(4):
        count = leaves >> level
        local_ref[base : base + count * rhs, :] = current.reshape(count * rhs, LANES)
        lasts.append(current[count - 3 :])
        firsts.append(current[:3])
        base += count * rhs
        current = up(current, matrix)
    for slot, edges in enumerate((lasts, firsts)):
        edge_ref[slot] = paired(jnp.concatenate(edges, axis=0)).reshape(6 * rhs, LANES)
    ends = [
        pltpu.make_async_copy(
            edge_ref.at[slot],
            target.at[pl.ds(data_rows, 6 * rhs), :],
            arrived.at[len(moves) + 2 + slot],
        )
        for slot, target in enumerate((pay_right_ref, pay_left_ref))
    ]
    for copy in ends:
        copy.start()
    message = packed(current[0], current[1])
    for peer in range(message_ref.shape[0] // rhs):
        message_ref[peer * rhs : (peer + 1) * rhs, :] = message
    lane = lax.broadcasted_iota(jnp.int32, (1, LANES), 1)
    starts = level_starts(total_leaves, levels)
    last = starts[-1] // LANES * LANES
    width = coupling_ref.shape[1] - last
    for level in range(levels):
        clusters = total_leaves >> level
        if starts[level] >= last:
            ids = jnp.concatenate(
                [
                    coupling_ref[:, last : last + width],
                    jnp.zeros((coupling_ref.shape[0], LANES - width), jnp.int32),
                ],
                axis=1,
            )
            targets = lane + (last - starts[level])
        else:
            count = leaves >> level if level < 4 else 2 * GROUP >> (level - 4)
            unit = device if level < 4 else device // GROUP
            tile = unit * count // LANES
            ids = coupling_ref[
                :, pl.ds(pl.multiple_of(starts[level] + tile * LANES, LANES), LANES)
            ]
            targets = lane + tile * LANES
        relative = (ids - targets) & (clusters - 1)
        for slot, shift_by in enumerate(OFFSETS):
            hits = jnp.where(relative == (shift_by & (clusters - 1)), 0.5**level, 0.0)
            counts_ref[4 * level + slot : 4 * level + slot + 1, :] = jnp.sum(
                hits, axis=0, keepdims=True
            )
    for copy in sent + ends:
        copy.wait()


def near_kernel(
    total_leaves, first, dev_ref, near_ref, own_ref, before_ref, after_ref, *rest
):
    out_ref, places, weights = rest[-3:]
    rhs = out_ref.shape[0]
    leaves = near_ref.shape[1]
    entries = near_ref.shape[0]
    targets = out_ref.shape[1] // LANES
    for part, ref in enumerate((before_ref, own_ref, after_ref)):
        rows = slice(part * leaves, (part + 1) * leaves)
        axes = [
            ref[leaves * (rhs + axis) : leaves * (rhs + axis + 1), :] - 0.5 for axis in range(3)
        ]
        for axis in range(3):
            places[axis, rows, :] = axes[axis]
        places[3, rows, :] = axes[1] * axes[1] + axes[2] * axes[2]

        def fill(leaf, carry, part=part, ref=ref):
            charge = ref[pl.ds(pl.multiple_of(leaf * rhs, rhs), rhs), :] * (0.25 / math.pi)
            weights[part * leaves + leaf] = jnp.concatenate(halves(charge), axis=0)
            return carry

        lax.fori_loop(0, leaves, fill, 0, unroll=8)

    device = dev_ref[0]
    half_cycle = total_leaves // 2

    def row_of(kind, slot):
        return places[kind, pl.ds(slot, 1), :]

    def one(step, carry):
        leaf = step + first
        target = device * leaves + leaf
        here = [row_of(kind, leaves + leaf) for kind in range(4)]
        size = here[0] * here[0] + (here[3] + DELTA * DELTA)
        table = jnp.concatenate(
            [-2.0 * here[0], -2.0 * here[1], -2.0 * here[2], size]
            + [jnp.zeros((4, LANES), jnp.float32)],
            axis=0,
        )
        columns = jnp.transpose(table)
        ax, ay, az, size = [
            jnp.broadcast_to(columns[:, kind : kind + 1], (LANES, LANES)) for kind in range(4)
        ]
        total = jnp.zeros((2 * rhs, 2 * LANES), jnp.float32)
        for pair in range(entries // 2):
            highs, lows, sides = [], [], []
            for entry in (2 * pair, 2 * pair + 1):
                window = (
                    (near_ref[entry, leaf] - target + half_cycle) & (total_leaves - 1)
                ) - half_cycle
                source = leaves + leaf + window
                qx = row_of(0, source) + window.astype(jnp.float32) * (1.0 / leaves)
                squared = qx * qx + row_of(3, source)
                value = lax.rsqrt(
                    ((size + squared) + ax * qx) + (ay * row_of(1, source) + az * row_of(2, source))
                )
                high, low = halves(value)
                highs.append(high)
                lows.append(low)
                sides.append(weights[source])
            piece = jnp.concatenate(
                [jnp.concatenate(highs, axis=1), jnp.concatenate(lows, axis=1)], axis=0
            )
            total = total + bf16_dot(jnp.concatenate(sides, axis=1), piece, ((1,), (1,)))
        half = total[:, :LANES] + total[:, LANES:]
        out_ref[:, pl.ds(pl.multiple_of(step * LANES, LANES), LANES)] = (
            half[0:rhs, :] + half[rhs : 2 * rhs, :]
        )
        return carry

    lax.fori_loop(0, targets, one, 0, unroll=8)


def couple(window, count, level, lane0, counts_ref, x_ref, row0, rows):
    for t in range(count):
        parts = [
            window(t + shift_by, slot) * counts_ref[4 * level + slot, lane0 + t]
            for slot, shift_by in enumerate(OFFSETS)
        ]
        where = slice(row0 + t * rows, row0 + (t + 1) * rows)
        x_ref[where, 0:LANES] = packed(parts[0], parts[1])
        x_ref[where, LANES : 2 * LANES] = packed(parts[2], parts[3])


def local_kernel(
    dev_ref, counts_ref, local_ref, before_ref, after_ref, stack_ref, out_ref, x_ref, edge_ref
):
    device = dev_ref[0]
    rhs = local_ref.shape[0] // 60
    start = before_ref.shape[0] - 6 * rhs
    for side, ref in enumerate((before_ref, after_ref)):
        for pair in range(6):
            both = ref[start + pair * rhs : start + (pair + 1) * rhs, :]
            edge_ref[side, 2 * pair], edge_ref[side, 2 * pair + 1] = unpacked(both)
    base = 0
    for level in range(4):
        count = 32 >> level

        def window(t, slot, count=count, base=base, level=level):
            if t < 0:
                return edge_ref[0, 3 * level + t + 3]
            if t >= count:
                return edge_ref[1, 3 * level + t - count]
            return local_ref[base + t * rhs : base + (t + 1) * rhs, :]

        lane0 = (device * count) & (LANES - 1)
        couple(window, count, level, lane0, counts_ref, x_ref, base, rhs)
        base += count * rhs
    terms = dot(x_ref[...], stack_ref[...])
    out_ref[...] = paired(terms.reshape(-1, rhs, LANES)).reshape(out_ref.shape)


def upper_kernel(
    total_leaves,
    dev_ref,
    counts_ref,
    gathered_ref,
    transfer_ref,
    stack_ref,
    paths_ref,
    _,
    out_ref,
    x_ref,
    top_ref,
    *sparse,
):
    device = dev_ref[0]
    index = device % GROUP
    group = device // GROUP
    rhs = out_ref.shape[0] // GROUP
    groups = gathered_ref.shape[0] // rhs
    matrix = up_matrix(transfer_ref)
    half = LANES // 2

    level9 = dot(gathered_ref[...], paths_ref[:, 4 * LANES :]).reshape(groups, rhs, LANES)
    level10 = up(level9, matrix)
    level11 = up(level10, matrix)
    top_ref[0:groups] = level9
    top_ref[groups : groups + groups // 2] = level10
    top_ref[groups + groups // 2 : groups + groups // 2 + groups // 4] = level11

    beside = [
        gathered_ref[pl.ds(pl.multiple_of(((group + step) & (groups - 1)) * rhs, 8), rhs), :]
        for step in range(-2, 3)
    ]
    for ref in sparse:
        ref[...] = jnp.zeros(ref.shape, jnp.float32)

    def place(ref, count, position, value):
        inside = (position >= -3) & (position < count + 3)
        ref[jnp.where(inside, position + 3, count + 6)] = value

    for step in (-1, 0, 1):
        for side, value in enumerate(unpacked(beside[step + 2])):
            place(sparse[0], 2 * GROUP, step * 2 * GROUP + 2 * index + side, value)
    nearby = dot(jnp.concatenate(beside, axis=0), paths_ref[:, : 4 * LANES])
    for level in range(5, 9):
        count = 2 * GROUP >> (level - 4)
        reach = (-1, 0, 1) if count >= 3 else (-2, -1, 0, 1, 2)
        for step in reach:
            place(
                sparse[level - 4],
                count,
                step * count + (index >> (level - 5)),
                nearby[(step + 2) * rhs : (step + 3) * rhs, (level - 5) * LANES :][:, :LANES],
            )

    row0 = 0
    spans = []
    for level in range(4, 9):
        count = 2 * GROUP >> (level - 4)
        ref = sparse[level - 4]
        lane0 = (group * count) & (LANES - 1)
        couple(
            lambda t, slot, ref=ref: ref[t + 3], count, level, lane0, counts_ref, x_ref, row0, rhs
        )
        spans.append((row0, count))
        row0 += count * rhs
    lane_base = LANES // 2
    top_base = 0
    for level in range(9, 12):
        clusters = groups >> (level - 9)
        cluster = group >> (level - 9)
        couple(
            lambda t, slot: top_ref[top_base + ((cluster + t) & (clusters - 1))],
            1,
            level,
            lane_base + cluster,
            counts_ref,
            x_ref,
            row0,
            rhs,
        )
        spans.append((row0, 1))
        row0 += rhs
        lane_base += clusters
        top_base += clusters
    terms = dot(x_ref[...], stack_ref[...])

    def term(level):
        start, count = spans[level - 4]
        return terms[start : start + count * rhs].reshape(count, rhs, LANES)

    current = term(11)[0]
    for level in (10, 9):
        child = (group >> (level - 9)) & 1
        current = term(level)[0] + down(current, transfer_ref[child])
    both = jnp.concatenate([transfer_ref[0], transfer_ref[1]], axis=0)
    current = (dot_t(current[:, :half], both) + paired(term(8))[0])[None]
    matrix = down_matrix(transfer_ref)
    for level in (7, 6, 5, 4):
        current = paired(term(level)) + down_pairs(current, matrix)
    out_ref[...] = current.reshape(out_ref.shape)


def final_kernel(
    parts_ref, terms_ref, transfer_ref, basis_ref, inverse_ref, near_a_ref, near_b_ref, out_ref
):
    rhs = out_ref.shape[0]
    leaves = inverse_ref.shape[0]
    total = parts_ref[0:rhs, :]
    for sender in range(1, GROUP):
        total = total + parts_ref[sender * rhs : (sender + 1) * rhs, :]
    current = total[None]
    matrix = down_matrix(transfer_ref)
    base = terms_ref.shape[0]
    for level in (3, 2, 1, 0):
        count = leaves >> level + 1
        base -= count * rhs
        mine = terms_ref[base : base + count * rhs, :].reshape(count, rhs, LANES)
        current = mine + down_pairs(current, matrix)
    lane = lax.broadcasted_iota(jnp.int32, (rhs, LANES), 1)
    low = lane < LANES // 2
    zero = jnp.zeros((rhs, LANES), jnp.float32)
    for four in range(leaves // 4):
        rows, sides = [], []
        for slot in range(4):
            leaf = 4 * four + slot
            value = jnp.where(low if slot % 2 == 0 else ~low, current[leaf // 2], 0.0)
            rows.append(jnp.concatenate([value, zero] if slot < 2 else [zero, value], axis=1))
            sides.append(basis_ref[:, leaf * LANES : (leaf + 1) * LANES])
        far = dot(jnp.concatenate(rows, axis=0), jnp.concatenate(sides, axis=0))
        for slot in range(4):
            leaf = 4 * four + slot
            ids = jnp.broadcast_to(inverse_ref[leaf : leaf + 1, :], (rhs, LANES))
            value = jnp.take_along_axis(far[slot * rhs : (slot + 1) * rhs], ids, axis=1)
            near_ref = near_a_ref if leaf < leaves // 2 else near_b_ref
            at = leaf % (leaves // 2) * LANES
            out_ref[:, leaf * LANES : (leaf + 1) * LANES] = value + near_ref[:, at : at + LANES]


def call(kernel, outs, scalars, operands, scratch=(), cost=None, kept=(), limit=VMEM_BYTES, far=0):
    smem = pl.BlockSpec(memory_space=pltpu.SMEM)
    vmem = pl.BlockSpec(memory_space=pltpu.VMEM)
    hbm = pl.BlockSpec(memory_space=pltpu.HBM)
    return pl.pallas_call(
        kernel,
        out_shape=outs,
        in_specs=[smem] * len(scalars) + [vmem] * len(operands) + [hbm] * len(kept),
        out_specs=[hbm] * far + [vmem] * (len(outs) - far) if isinstance(outs, list) else vmem,
        scratch_shapes=list(scratch),
        cost_estimate=cost,
        compiler_params=pltpu.CompilerParams(vmem_limit_bytes=limit),
    )(*scalars, *operands, *kept)


def local(points, charges, basis, transfer, near_list, coupling_list, ordering):
    devices = lax.axis_size("leaf")
    device = jnp.reshape(lax.axis_index("leaf"), (1,)).astype(jnp.int32)
    leaves = near_list.shape[1]
    rhs = charges.shape[0]
    total_leaves = leaves * devices
    levels = total_leaves.bit_length() - 3
    groups = devices // GROUP
    f32 = jnp.float32
    ids = ordering.reshape(leaves, LANES)
    stack = jnp.asarray(coupling_stack())
    data_rows = leaves * (rhs + 3)
    pay_rows = data_rows + 6 * rhs
    local_rows = (leaves * 2 - 4) * rhs

    inputs = [points, charges, basis, ids, transfer, coupling_list]
    pay_right, pay_left, message, local_terms, counts, inverse, paths = call(
        lambda *refs: prepare_kernel(total_leaves, levels, *refs),
        [
            jax.ShapeDtypeStruct((pay_rows, LANES), f32),
            jax.ShapeDtypeStruct((pay_rows, LANES), f32),
            jax.ShapeDtypeStruct((groups * rhs, LANES), f32),
            jax.ShapeDtypeStruct((local_rows, LANES), f32),
            jax.ShapeDtypeStruct((4 * levels, LANES), f32),
            jax.ShapeDtypeStruct((leaves, LANES), jnp.int32),
            jax.ShapeDtypeStruct((LANES, 5 * LANES), f32),
        ],
        [device],
        [],
        [
            *[pltpu.VMEM(array.shape, array.dtype) for array in inputs],
            pltpu.VMEM((data_rows, LANES), f32),
            pltpu.VMEM((2, 6 * rhs, LANES), f32),
            pltpu.SemaphoreType.DMA((len(inputs) + 4,)),
        ],
        kept=inputs,
        limit=FIRST_BYTES,
        far=2,
    )
    before = lax.ppermute(pay_right, "leaf", [(i, (i + 1) % devices) for i in range(devices)])
    after = lax.ppermute(pay_left, "leaf", [((i + 1) % devices, i) for i in range(devices)])
    gathered = lax.all_to_all(
        message,
        "leaf",
        0,
        0,
        axis_index_groups=[[g * GROUP + i for g in range(groups)] for i in range(GROUP)],
        tiled=True,
    )

    def near(first, count, extra):
        return call(
            lambda *refs: near_kernel(total_leaves, first, *refs),
            jax.ShapeDtypeStruct((rhs, count * LANES), f32),
            [device, near_list],
            [pay_right, before, after],
            [
                pltpu.VMEM((4, 3 * leaves, LANES), f32),
                pltpu.VMEM((3 * leaves, 2 * rhs, LANES), jnp.bfloat16),
            ],
            pl.CostEstimate(
                flops=count * 12 * 128 * 128 * 100,
                bytes_accessed=8 << 20,
                transcendentals=count * 12 * 128 * 128,
            ),
            kept=extra,
        )

    near_a = near(0, leaves // 2, [])
    terms = call(
        local_kernel,
        jax.ShapeDtypeStruct((local_rows // 2, LANES), f32),
        [device, counts],
        [local_terms, before, after, stack],
        [pltpu.VMEM((local_rows, 2 * LANES), f32), pltpu.VMEM((2, 12, rhs, LANES), f32)],
    )
    upper_rows = (4 * GROUP - 2 + 3) * rhs
    spread = call(
        lambda *refs: upper_kernel(total_leaves, *refs),
        jax.ShapeDtypeStruct((GROUP * rhs, LANES), f32),
        [device, counts],
        [gathered, transfer, stack, paths],
        [
            pltpu.VMEM((upper_rows, 2 * LANES), f32),
            pltpu.VMEM((2 * groups, rhs, LANES), f32),
            *[
                pltpu.VMEM(((2 * GROUP >> step) + 7, rhs, LANES), f32)
                for step in range(5)
            ],
        ],
        kept=[near_a],
    )
    parts = lax.all_to_all(
        spread,
        "leaf",
        0,
        0,
        axis_index_groups=[[g * GROUP + i for i in range(GROUP)] for g in range(groups)],
        tiled=True,
    )
    near_b = near(leaves // 2, leaves // 2, [spread])
    return call(
        final_kernel,
        jax.ShapeDtypeStruct(charges.shape, f32),
        [],
        [parts, terms, transfer, basis, inverse, near_a, near_b],
    )


def solution(mesh):
    placed = (
        P(None, "leaf"),
        P(None, "leaf"),
        P(None, "leaf"),
        P(),
        P(None, "leaf"),
        P(),
        P("leaf"),
    )
    return jax.shard_map(
        local, mesh=mesh, in_specs=placed, out_specs=P(None, "leaf"), check_vma=False
    )
```

```python
import math

import jax
import jax.numpy as jnp
import numpy as np
from jax import lax
from jax.experimental import pallas as pl
from jax.experimental.pallas import tpu as pltpu
from jax.sharding import PartitionSpec as P

ORDER = 4
OFFSETS = (2, 3, -3, -2)
DELTA = 0.05
PROXY = 0.35
GROUP = 16
LANES = 128
VMEM_BYTES = 50 * 1024 * 1024
FIRST_BYTES = 61 * 1024 * 1024


def coupling_stack():
    nodes = np.cos((2.0 * np.arange(ORDER) + 1.0) * (math.pi / (2.0 * ORDER)))
    grid = np.stack(np.meshgrid(nodes, nodes, nodes, indexing="ij")).reshape(3, -1) * PROXY
    stacked = []
    for shift_by in OFFSETS:
        moved = grid + np.array([float(shift_by), 0.0, 0.0])[:, None]
        difference = grid[:, :, None] - moved[:, None, :]
        stacked.append((0.25 / math.pi / np.sqrt((difference**2).sum(0))).T)
    table = np.concatenate(stacked, axis=0)
    return np.concatenate([table, table], axis=1).astype(np.float32)


def halves(value):
    high = value.astype(jnp.bfloat16)
    return high, (value - high.astype(jnp.float32)).astype(jnp.bfloat16)


def bf16_dot(left, right, dims):
    return lax.dot_general(left, right, (dims, ((), ())), preferred_element_type=jnp.float32)


def summed(product, rows, columns):
    return product[:rows, :columns] + (product[:rows, columns:] + product[rows:, :columns])


def dot(left, right):
    both = bf16_dot(
        jnp.concatenate(halves(left), axis=0), jnp.concatenate(halves(right), axis=1), ((1,), (0,))
    )
    return summed(both, left.shape[0], right.shape[1])


def dot_t(left, right):
    both = bf16_dot(
        jnp.concatenate(halves(left), axis=0), jnp.concatenate(halves(right), axis=0), ((1,), (1,))
    )
    return summed(both, left.shape[0], right.shape[0])


def first_half(shape):
    return lax.broadcasted_iota(jnp.int32, shape, len(shape) - 1) < LANES // 2


def packed(left, right):
    return jnp.where(first_half(left.shape), left, right)


def unpacked(both):
    turned = pltpu.roll(both, LANES // 2, 1)
    return packed(both, turned), packed(turned, both)


def twice(matrix):
    return jnp.concatenate([matrix, matrix], axis=1)


def up_matrix(transfer_ref):
    return jnp.concatenate([twice(transfer_ref[0]), twice(transfer_ref[1])], axis=0)


def up(values, matrix):
    count, rows, lanes = values.shape
    both = paired(values).reshape(count // 2 * rows, lanes)
    return dot(both, matrix).reshape(count // 2, rows, lanes)


def down(parent, matrix):
    doubled = jnp.concatenate([matrix, matrix], axis=0)
    return dot_t(parent[:, : LANES // 2], doubled)


def down_matrix(transfer_ref):
    both = jnp.concatenate([transfer_ref[0], transfer_ref[1]], axis=0)
    zero = jnp.zeros(both.shape, jnp.float32)
    return jnp.concatenate(
        [jnp.concatenate([both, zero], axis=1), jnp.concatenate([zero, both], axis=1)], axis=0
    )


def down_pairs(pairs, matrix):
    count, rows, lanes = pairs.shape
    both = dot_t(pairs.reshape(count * rows, lanes), matrix).reshape(count, rows, 2 * lanes)
    return jnp.stack([both[:, :, :lanes], both[:, :, lanes:]], axis=1).reshape(
        2 * count, rows, lanes
    )


def paired(values):
    count, rows, lanes = values.shape
    pairs = values.reshape(count // 2, 2, rows, lanes)
    return packed(pairs[:, 0], pairs[:, 1])


def level_starts(total_leaves, levels):
    return [2 * total_leaves - 2 * (total_leaves >> level) for level in range(levels)]


def expand_kernel(
    points_in,
    charges_in,
    basis_in,
    ordering_in,
    transfer_in,
    pay_right_ref,
    pay_left_ref,
    message_ref,
    local_ref,
    points_ref,
    charges_ref,
    basis_ref,
    ordering_ref,
    transfer_ref,
    data_ref,
    edge_ref,
    arrived,
):
    moves = [
        (charges_in, charges_ref),
        (points_in, points_ref),
        (ordering_in, ordering_ref),
        (transfer_in, transfer_ref),
        (basis_in, basis_ref),
    ]
    copies = [
        pltpu.make_async_copy(source, target, arrived.at[slot])
        for slot, (source, target) in enumerate(moves)
    ]
    for copy in copies:
        copy.start()
    rhs = charges_ref.shape[0]
    leaves = ordering_ref.shape[0]
    data_rows = leaves * (rhs + 3)
    copies[0].wait()
    copies[1].wait()
    for leaf in range(leaves):
        cols = slice(leaf * LANES, (leaf + 1) * LANES)
        data_ref[leaf * rhs : (leaf + 1) * rhs, :] = charges_ref[:, cols]
        for axis in range(3):
            at = leaves * (rhs + axis) + leaf
            data_ref[at : at + 1, :] = points_ref[axis : axis + 1, cols]
    sent = [
        pltpu.make_async_copy(
            data_ref, target.at[pl.ds(0, data_rows), :], arrived.at[len(moves) + slot]
        )
        for slot, target in enumerate((pay_right_ref, pay_left_ref))
    ]
    for copy in sent:
        copy.start()
    zero = jnp.zeros((rhs, LANES), jnp.float32)
    expansions = []
    for copy in copies[2:]:
        copy.wait()
    for pair in range(leaves // 2):
        gathered = []
        for leaf in (2 * pair, 2 * pair + 1):
            ids = jnp.broadcast_to(ordering_ref[leaf : leaf + 1, :], (rhs, LANES))
            cols = slice(leaf * LANES, (leaf + 1) * LANES)
            gathered.append(jnp.take_along_axis(charges_ref[:, cols], ids, axis=1))
        left = jnp.concatenate(
            [
                jnp.concatenate([gathered[0], zero], axis=1),
                jnp.concatenate([zero, gathered[1]], axis=1),
            ],
            axis=0,
        )
        part = basis_ref[:, 2 * pair * LANES : (2 * pair + 2) * LANES]
        both = dot_t(left, jnp.concatenate([part, part], axis=0))
        expansions.append(both.reshape(2, rhs, LANES))
    current = jnp.concatenate(expansions, axis=0)
    matrix = up_matrix(transfer_ref)
    base = 0
    lasts, firsts = [], []
    for level in range(4):
        count = leaves >> level
        local_ref[base : base + count * rhs, :] = current.reshape(count * rhs, LANES)
        lasts.append(current[count - 3 :])
        firsts.append(current[:3])
        base += count * rhs
        current = up(current, matrix)
    for slot, edges in enumerate((lasts, firsts)):
        edge_ref[slot] = paired(jnp.concatenate(edges, axis=0)).reshape(6 * rhs, LANES)
    ends = [
        pltpu.make_async_copy(
            edge_ref.at[slot],
            target.at[pl.ds(data_rows, 6 * rhs), :],
            arrived.at[len(moves) + 2 + slot],
        )
        for slot, target in enumerate((pay_right_ref, pay_left_ref))
    ]
    for copy in ends:
        copy.start()
    message = packed(current[0], current[1])
    for peer in range(message_ref.shape[0] // rhs):
        message_ref[peer * rhs : (peer + 1) * rhs, :] = message
    for copy in sent + ends:
        copy.wait()


def tables_kernel(
    total_leaves,
    levels,
    dev_ref,
    ordering_ref,
    transfer_ref,
    coupling_ref,
    _,
    counts_ref,
    inverse_ref,
    paths_ref,
):
    device = dev_ref[0]
    leaves = ordering_ref.shape[0]
    slots = lax.broadcasted_iota(jnp.int32, (LANES, LANES), 0)
    numbers = lax.broadcasted_iota(jnp.int32, (16, LANES), 1).astype(jnp.float32)
    numbers = numbers.astype(jnp.bfloat16)
    for leaf in range(leaves):
        hit = jnp.where(ordering_ref[leaf : leaf + 1, :] == slots, 1.0, 0.0).astype(jnp.bfloat16)
        found = bf16_dot(numbers, hit, ((1,), (1,)))
        inverse_ref[leaf : leaf + 1, :] = found[0:1].astype(jnp.int32)
    path = up_matrix(transfer_ref)
    for level in range(5, 10):
        paths_ref[:, (level - 5) * LANES : (level - 4) * LANES] = path
        if level < 9:
            bit = ((device % GROUP) >> (level - 5)) & 1
            path = dot(path[:, : LANES // 2], twice(transfer_ref[bit]))
    lane = lax.broadcasted_iota(jnp.int32, (1, LANES), 1)
    starts = level_starts(total_leaves, levels)
    last = starts[-1] // LANES * LANES
    width = coupling_ref.shape[1] - last
    for level in range(levels):
        clusters = total_leaves >> level
        if starts[level] >= last:
            ids = jnp.concatenate(
                [
                    coupling_ref[:, last : last + width],
                    jnp.zeros((coupling_ref.shape[0], LANES - width), jnp.int32),
                ],
                axis=1,
            )
            targets = lane + (last - starts[level])
        else:
            count = leaves >> level if level < 4 else 2 * GROUP >> (level - 4)
            unit = device if level < 4 else device // GROUP
            tile = unit * count // LANES
            ids = coupling_ref[
                :, pl.ds(pl.multiple_of(starts[level] + tile * LANES, LANES), LANES)
            ]
            targets = lane + tile * LANES
        relative = (ids - targets) & (clusters - 1)
        for slot, shift_by in enumerate(OFFSETS):
            hits = jnp.where(relative == (shift_by & (clusters - 1)), 0.5**level, 0.0)
            counts_ref[4 * level + slot : 4 * level + slot + 1, :] = jnp.sum(
                hits, axis=0, keepdims=True
            )


def near_kernel(
    total_leaves, dev_ref, near_ref, own_ref, before_ref, after_ref, *rest
):
    out_ref, places, weights = rest[-3:]
    rhs = out_ref.shape[0]
    leaves = near_ref.shape[1]
    entries = near_ref.shape[0]
    for part, ref in enumerate((before_ref, own_ref, after_ref)):
        rows = slice(part * leaves, (part + 1) * leaves)
        axes = [
            ref[leaves * (rhs + axis) : leaves * (rhs + axis + 1), :] - 0.5 for axis in range(3)
        ]
        for axis in range(3):
            places[axis, rows, :] = axes[axis]
        places[3, rows, :] = axes[1] * axes[1] + axes[2] * axes[2]

        def fill(leaf, carry, part=part, ref=ref):
            charge = ref[pl.ds(pl.multiple_of(leaf * rhs, rhs), rhs), :] * (0.25 / math.pi)
            weights[part * leaves + leaf] = jnp.concatenate(halves(charge), axis=0)
            return carry

        lax.fori_loop(0, leaves, fill, 0, unroll=8)

    device = dev_ref[0]
    half_cycle = total_leaves // 2

    def row_of(kind, slot):
        return places[kind, pl.ds(slot, 1), :]

    def one(leaf, carry):
        target = device * leaves + leaf
        here = [row_of(kind, leaves + leaf) for kind in range(4)]
        size = here[0] * here[0] + (here[3] + DELTA * DELTA)
        table = jnp.concatenate(
            [-2.0 * here[0], -2.0 * here[1], -2.0 * here[2], size]
            + [jnp.zeros((4, LANES), jnp.float32)],
            axis=0,
        )
        columns = jnp.transpose(table)
        ax, ay, az, size = [
            jnp.broadcast_to(columns[:, kind : kind + 1], (LANES, LANES)) for kind in range(4)
        ]
        total = jnp.zeros((2 * rhs, 2 * LANES), jnp.float32)
        for pair in range(entries // 2):
            highs, lows, sides = [], [], []
            for entry in (2 * pair, 2 * pair + 1):
                window = (
                    (near_ref[entry, leaf] - target + half_cycle) & (total_leaves - 1)
                ) - half_cycle
                source = leaves + leaf + window
                qx = row_of(0, source) + window.astype(jnp.float32) * (1.0 / leaves)
                squared = qx * qx + row_of(3, source)
                value = lax.rsqrt(
                    ((size + squared) + ax * qx) + (ay * row_of(1, source) + az * row_of(2, source))
                )
                high, low = halves(value)
                highs.append(high)
                lows.append(low)
                sides.append(weights[source])
            piece = jnp.concatenate(
                [jnp.concatenate(highs, axis=1), jnp.concatenate(lows, axis=1)], axis=0
            )
            total = total + bf16_dot(jnp.concatenate(sides, axis=1), piece, ((1,), (1,)))
        half = total[:, :LANES] + total[:, LANES:]
        out_ref[:, pl.ds(pl.multiple_of(leaf * LANES, LANES), LANES)] = (
            half[0:rhs, :] + half[rhs : 2 * rhs, :]
        )
        return carry

    lax.fori_loop(0, leaves, one, 0, unroll=8)


def couple(window, count, level, lane0, counts_ref, x_ref, row0, rows):
    for t in range(count):
        parts = [
            window(t + shift_by, slot) * counts_ref[4 * level + slot, lane0 + t]
            for slot, shift_by in enumerate(OFFSETS)
        ]
        where = slice(row0 + t * rows, row0 + (t + 1) * rows)
        x_ref[where, 0:LANES] = packed(parts[0], parts[1])
        x_ref[where, LANES : 2 * LANES] = packed(parts[2], parts[3])


def local_kernel(
    dev_ref, counts_ref, local_ref, before_ref, after_ref, stack_ref, out_ref, x_ref, edge_ref
):
    device = dev_ref[0]
    rhs = local_ref.shape[0] // 60
    start = before_ref.shape[0] - 6 * rhs
    for side, ref in enumerate((before_ref, after_ref)):
        for pair in range(6):
            both = ref[start + pair * rhs : start + (pair + 1) * rhs, :]
            edge_ref[side, 2 * pair], edge_ref[side, 2 * pair + 1] = unpacked(both)
    base = 0
    for level in range(4):
        count = 32 >> level

        def window(t, slot, count=count, base=base, level=level):
            if t < 0:
                return edge_ref[0, 3 * level + t + 3]
            if t >= count:
                return edge_ref[1, 3 * level + t - count]
            return local_ref[base + t * rhs : base + (t + 1) * rhs, :]

        lane0 = (device * count) & (LANES - 1)
        couple(window, count, level, lane0, counts_ref, x_ref, base, rhs)
        base += count * rhs
    terms = dot(x_ref[...], stack_ref[...])
    out_ref[...] = paired(terms.reshape(-1, rhs, LANES)).reshape(out_ref.shape)


def upper_kernel(
    total_leaves,
    dev_ref,
    counts_ref,
    gathered_ref,
    transfer_ref,
    stack_ref,
    paths_ref,
    out_ref,
    x_ref,
    top_ref,
    *sparse,
):
    device = dev_ref[0]
    index = device % GROUP
    group = device // GROUP
    rhs = out_ref.shape[0] // GROUP
    groups = gathered_ref.shape[0] // rhs
    matrix = up_matrix(transfer_ref)
    half = LANES // 2

    level9 = dot(gathered_ref[...], paths_ref[:, 4 * LANES :]).reshape(groups, rhs, LANES)
    level10 = up(level9, matrix)
    level11 = up(level10, matrix)
    top_ref[0:groups] = level9
    top_ref[groups : groups + groups // 2] = level10
    top_ref[groups + groups // 2 : groups + groups // 2 + groups // 4] = level11

    beside = [
        gathered_ref[pl.ds(pl.multiple_of(((group + step) & (groups - 1)) * rhs, 8), rhs), :]
        for step in range(-2, 3)
    ]
    for ref in sparse:
        ref[...] = jnp.zeros(ref.shape, jnp.float32)

    def place(ref, count, position, value):
        inside = (position >= -3) & (position < count + 3)
        ref[jnp.where(inside, position + 3, count + 6)] = value

    for step in (-1, 0, 1):
        for side, value in enumerate(unpacked(beside[step + 2])):
            place(sparse[0], 2 * GROUP, step * 2 * GROUP + 2 * index + side, value)
    nearby = dot(jnp.concatenate(beside, axis=0), paths_ref[:, : 4 * LANES])
    for level in range(5, 9):
        count = 2 * GROUP >> (level - 4)
        reach = (-1, 0, 1) if count >= 3 else (-2, -1, 0, 1, 2)
        for step in reach:
            place(
                sparse[level - 4],
                count,
                step * count + (index >> (level - 5)),
                nearby[(step + 2) * rhs : (step + 3) * rhs, (level - 5) * LANES :][:, :LANES],
            )

    row0 = 0
    spans = []
    for level in range(4, 9):
        count = 2 * GROUP >> (level - 4)
        ref = sparse[level - 4]
        lane0 = (group * count) & (LANES - 1)
        couple(
            lambda t, slot, ref=ref: ref[t + 3], count, level, lane0, counts_ref, x_ref, row0, rhs
        )
        spans.append((row0, count))
        row0 += count * rhs
    lane_base = LANES // 2
    top_base = 0
    for level in range(9, 12):
        clusters = groups >> (level - 9)
        cluster = group >> (level - 9)
        couple(
            lambda t, slot: top_ref[top_base + ((cluster + t) & (clusters - 1))],
            1,
            level,
            lane_base + cluster,
            counts_ref,
            x_ref,
            row0,
            rhs,
        )
        spans.append((row0, 1))
        row0 += rhs
        lane_base += clusters
        top_base += clusters
    terms = dot(x_ref[...], stack_ref[...])

    def term(level):
        start, count = spans[level - 4]
        return terms[start : start + count * rhs].reshape(count, rhs, LANES)

    current = term(11)[0]
    for level in (10, 9):
        child = (group >> (level - 9)) & 1
        current = term(level)[0] + down(current, transfer_ref[child])
    both = jnp.concatenate([transfer_ref[0], transfer_ref[1]], axis=0)
    current = (dot_t(current[:, :half], both) + paired(term(8))[0])[None]
    matrix = down_matrix(transfer_ref)
    for level in (7, 6, 5, 4):
        current = paired(term(level)) + down_pairs(current, matrix)
    out_ref[...] = current.reshape(out_ref.shape)


def final_kernel(
    parts_ref, terms_ref, transfer_ref, basis_ref, inverse_ref, near_ref, out_ref
):
    rhs = out_ref.shape[0]
    leaves = inverse_ref.shape[0]
    total = parts_ref[0:rhs, :]
    for sender in range(1, GROUP):
        total = total + parts_ref[sender * rhs : (sender + 1) * rhs, :]
    current = total[None]
    matrix = down_matrix(transfer_ref)
    base = terms_ref.shape[0]
    for level in (3, 2, 1, 0):
        count = leaves >> level + 1
        base -= count * rhs
        mine = terms_ref[base : base + count * rhs, :].reshape(count, rhs, LANES)
        current = mine + down_pairs(current, matrix)
    lane = lax.broadcasted_iota(jnp.int32, (rhs, LANES), 1)
    low = lane < LANES // 2
    zero = jnp.zeros((rhs, LANES), jnp.float32)
    for four in range(leaves // 4):
        rows, sides = [], []
        for slot in range(4):
            leaf = 4 * four + slot
            value = jnp.where(low if slot % 2 == 0 else ~low, current[leaf // 2], 0.0)
            rows.append(jnp.concatenate([value, zero] if slot < 2 else [zero, value], axis=1))
            sides.append(basis_ref[:, leaf * LANES : (leaf + 1) * LANES])
        far = dot(jnp.concatenate(rows, axis=0), jnp.concatenate(sides, axis=0))
        for slot in range(4):
            leaf = 4 * four + slot
            ids = jnp.broadcast_to(inverse_ref[leaf : leaf + 1, :], (rhs, LANES))
            value = jnp.take_along_axis(far[slot * rhs : (slot + 1) * rhs], ids, axis=1)
            cols = slice(leaf * LANES, (leaf + 1) * LANES)
            out_ref[:, cols] = value + near_ref[:, cols]


def call(kernel, outs, scalars, operands, scratch=(), cost=None, kept=(), limit=VMEM_BYTES, far=0):
    smem = pl.BlockSpec(memory_space=pltpu.SMEM)
    vmem = pl.BlockSpec(memory_space=pltpu.VMEM)
    hbm = pl.BlockSpec(memory_space=pltpu.HBM)
    return pl.pallas_call(
        kernel,
        out_shape=outs,
        in_specs=[smem] * len(scalars) + [vmem] * len(operands) + [hbm] * len(kept),
        out_specs=[hbm] * far + [vmem] * (len(outs) - far) if isinstance(outs, list) else vmem,
        scratch_shapes=list(scratch),
        cost_estimate=cost,
        compiler_params=pltpu.CompilerParams(vmem_limit_bytes=limit),
    )(*scalars, *operands, *kept)


def local(points, charges, basis, transfer, near_list, coupling_list, ordering):
    devices = lax.axis_size("leaf")
    device = jnp.reshape(lax.axis_index("leaf"), (1,)).astype(jnp.int32)
    leaves = near_list.shape[1]
    rhs = charges.shape[0]
    total_leaves = leaves * devices
    levels = total_leaves.bit_length() - 3
    groups = devices // GROUP
    f32 = jnp.float32
    ids = ordering.reshape(leaves, LANES)
    stack = jnp.asarray(coupling_stack())
    data_rows = leaves * (rhs + 3)
    pay_rows = data_rows + 6 * rhs
    local_rows = (leaves * 2 - 4) * rhs

    inputs = [points, charges, basis, ids, transfer]
    pay_right, pay_left, message, local_terms = call(
        expand_kernel,
        [
            jax.ShapeDtypeStruct((pay_rows, LANES), f32),
            jax.ShapeDtypeStruct((pay_rows, LANES), f32),
            jax.ShapeDtypeStruct((groups * rhs, LANES), f32),
            jax.ShapeDtypeStruct((local_rows, LANES), f32),
        ],
        [],
        [],
        [
            *[pltpu.VMEM(array.shape, array.dtype) for array in inputs],
            pltpu.VMEM((data_rows, LANES), f32),
            pltpu.VMEM((2, 6 * rhs, LANES), f32),
            pltpu.SemaphoreType.DMA((len(inputs) + 4,)),
        ],
        kept=inputs,
        limit=FIRST_BYTES,
        far=2,
    )
    counts, inverse, paths = call(
        lambda *refs: tables_kernel(total_leaves, levels, *refs),
        [
            jax.ShapeDtypeStruct((4 * levels, LANES), f32),
            jax.ShapeDtypeStruct((leaves, LANES), jnp.int32),
            jax.ShapeDtypeStruct((LANES, 5 * LANES), f32),
        ],
        [device],
        [ids, transfer, coupling_list],
        cost=pl.CostEstimate(flops=1 << 28, bytes_accessed=2 << 20, transcendentals=0),
        kept=[message],
    )
    before = lax.ppermute(pay_right, "leaf", [(i, (i + 1) % devices) for i in range(devices)])
    after = lax.ppermute(pay_left, "leaf", [((i + 1) % devices, i) for i in range(devices)])
    gathered = lax.all_to_all(
        message,
        "leaf",
        0,
        0,
        axis_index_groups=[[g * GROUP + i for g in range(groups)] for i in range(GROUP)],
        tiled=True,
    )

    terms = call(
        local_kernel,
        jax.ShapeDtypeStruct((local_rows // 2, LANES), f32),
        [device, counts],
        [local_terms, before, after, stack],
        [pltpu.VMEM((local_rows, 2 * LANES), f32), pltpu.VMEM((2, 12, rhs, LANES), f32)],
    )
    upper_rows = (4 * GROUP - 2 + 3) * rhs
    spread = call(
        lambda *refs: upper_kernel(total_leaves, *refs),
        jax.ShapeDtypeStruct((GROUP * rhs, LANES), f32),
        [device, counts],
        [gathered, transfer, stack, paths],
        [
            pltpu.VMEM((upper_rows, 2 * LANES), f32),
            pltpu.VMEM((2 * groups, rhs, LANES), f32),
            *[
                pltpu.VMEM(((2 * GROUP >> step) + 7, rhs, LANES), f32)
                for step in range(5)
            ],
        ],
    )
    parts = lax.all_to_all(
        spread,
        "leaf",
        0,
        0,
        axis_index_groups=[[g * GROUP + i for i in range(GROUP)] for g in range(groups)],
        tiled=True,
    )
    near = call(
        lambda *refs: near_kernel(total_leaves, *refs),
        jax.ShapeDtypeStruct((rhs, leaves * LANES), f32),
        [device, near_list],
        [pay_right, before, after],
        [
            pltpu.VMEM((4, 3 * leaves, LANES), f32),
            pltpu.VMEM((3 * leaves, 2 * rhs, LANES), jnp.bfloat16),
        ],
        pl.CostEstimate(
            flops=leaves * 12 * 128 * 128 * 100,
            bytes_accessed=8 << 20,
            transcendentals=leaves * 12 * 128 * 128,
        ),
        kept=[spread],
    )
    return call(
        final_kernel,
        jax.ShapeDtypeStruct(charges.shape, f32),
        [],
        [parts, terms, transfer, basis, inverse, near],
    )


def solution(mesh):
    placed = (
        P(None, "leaf"),
        P(None, "leaf"),
        P(None, "leaf"),
        P(),
        P(None, "leaf"),
        P(),
        P("leaf"),
    )
    return jax.shard_map(
        local, mesh=mesh, in_specs=placed, out_specs=P(None, "leaf"), check_vma=False
    )
```

```python
import math

import jax
import jax.numpy as jnp
import numpy as np
from jax import lax
from jax.experimental import pallas as pl
from jax.experimental.pallas import tpu as pltpu
from jax.sharding import PartitionSpec as P

ORDER = 4
OFFSETS = (2, 3, -3, -2)
DELTA = 0.05
PROXY = 0.35
GROUP = 16
LANES = 128
TOP = GROUP.bit_length() + 4
VMEM_BYTES = 50 * 1024 * 1024
FIRST_BYTES = 61 * 1024 * 1024


def coupling_stack():
    nodes = np.cos((2.0 * np.arange(ORDER) + 1.0) * (math.pi / (2.0 * ORDER)))
    grid = np.stack(np.meshgrid(nodes, nodes, nodes, indexing="ij")).reshape(3, -1) * PROXY
    stacked = []
    for shift_by in OFFSETS:
        moved = grid + np.array([float(shift_by), 0.0, 0.0])[:, None]
        difference = grid[:, :, None] - moved[:, None, :]
        stacked.append((0.25 / math.pi / np.sqrt((difference**2).sum(0))).T)
    table = np.concatenate(stacked, axis=0)
    return np.concatenate([table, table], axis=1).astype(np.float32)


def halves(value):
    high = value.astype(jnp.bfloat16)
    return high, (value - high.astype(jnp.float32)).astype(jnp.bfloat16)


def bf16_dot(left, right, dims):
    return lax.dot_general(left, right, (dims, ((), ())), preferred_element_type=jnp.float32)


def summed(product, rows, columns):
    return product[:rows, :columns] + (product[:rows, columns:] + product[rows:, :columns])


def dot(left, right):
    both = bf16_dot(
        jnp.concatenate(halves(left), axis=0), jnp.concatenate(halves(right), axis=1), ((1,), (0,))
    )
    return summed(both, left.shape[0], right.shape[1])


def dot_t(left, right):
    both = bf16_dot(
        jnp.concatenate(halves(left), axis=0), jnp.concatenate(halves(right), axis=0), ((1,), (1,))
    )
    return summed(both, left.shape[0], right.shape[0])


def first_half(shape):
    return lax.broadcasted_iota(jnp.int32, shape, len(shape) - 1) < LANES // 2


def packed(left, right):
    return jnp.where(first_half(left.shape), left, right)


def unpacked(both):
    turned = pltpu.roll(both, LANES // 2, 1)
    return packed(both, turned), packed(turned, both)


def twice(matrix):
    return jnp.concatenate([matrix, matrix], axis=1)


def up_matrix(transfer_ref):
    return jnp.concatenate([twice(transfer_ref[0]), twice(transfer_ref[1])], axis=0)


def up(values, matrix):
    count, rows, lanes = values.shape
    both = paired(values).reshape(count // 2 * rows, lanes)
    return dot(both, matrix).reshape(count // 2, rows, lanes)


def down(parent, matrix):
    doubled = jnp.concatenate([matrix, matrix], axis=0)
    return dot_t(parent[:, : LANES // 2], doubled)


def down_matrix(transfer_ref):
    both = jnp.concatenate([transfer_ref[0], transfer_ref[1]], axis=0)
    zero = jnp.zeros(both.shape, jnp.float32)
    return jnp.concatenate(
        [jnp.concatenate([both, zero], axis=1), jnp.concatenate([zero, both], axis=1)], axis=0
    )


def down_pairs(pairs, matrix):
    count, rows, lanes = pairs.shape
    both = dot_t(pairs.reshape(count * rows, lanes), matrix).reshape(count, rows, 2 * lanes)
    return jnp.stack([both[:, :, :lanes], both[:, :, lanes:]], axis=1).reshape(
        2 * count, rows, lanes
    )


def paired(values):
    count, rows, lanes = values.shape
    pairs = values.reshape(count // 2, 2, rows, lanes)
    return packed(pairs[:, 0], pairs[:, 1])


def level_starts(total_leaves, levels):
    return [2 * total_leaves - 2 * (total_leaves >> level) for level in range(levels)]


def expand_kernel(
    charges_in,
    ordering_in,
    basis_in,
    transfer_in,
    local_out,
    message_ref,
    charges_ref,
    ordering_ref,
    basis_ref,
    transfer_ref,
    local_ref,
    arrived,
):
    moves = [
        (charges_in, charges_ref),
        (ordering_in, ordering_ref),
        (basis_in, basis_ref),
        (transfer_in, transfer_ref),
    ]
    copies = [
        pltpu.make_async_copy(source, target, arrived.at[slot])
        for slot, (source, target) in enumerate(moves)
    ]
    for copy in copies:
        copy.start()
    for copy in copies:
        copy.wait()
    rhs = charges_ref.shape[0]
    leaves = ordering_ref.shape[0]
    zero = jnp.zeros((rhs, LANES), jnp.float32)
    expansions = []
    for pair in range(leaves // 2):
        gathered = []
        for leaf in (2 * pair, 2 * pair + 1):
            ids = jnp.broadcast_to(ordering_ref[leaf : leaf + 1, :], (rhs, LANES))
            cols = slice(leaf * LANES, (leaf + 1) * LANES)
            gathered.append(jnp.take_along_axis(charges_ref[:, cols], ids, axis=1))
        left = jnp.concatenate(
            [
                jnp.concatenate([gathered[0], zero], axis=1),
                jnp.concatenate([zero, gathered[1]], axis=1),
            ],
            axis=0,
        )
        part = basis_ref[:, 2 * pair * LANES : (2 * pair + 2) * LANES]
        both = dot_t(left, jnp.concatenate([part, part], axis=0))
        expansions.append(both.reshape(2, rhs, LANES))
    current = jnp.concatenate(expansions, axis=0)
    matrix = up_matrix(transfer_ref)
    base = 0
    sent = []
    for level in range(4):
        size = (leaves >> level) * rhs
        local_ref[base : base + size, :] = current.reshape(size, LANES)
        rows = pl.ds(base, size)
        copy = pltpu.make_async_copy(
            local_ref.at[rows, :], local_out.at[rows, :], arrived.at[len(moves) + level]
        )
        copy.start()
        sent.append(copy)
        base += size
        current = up(current, matrix)
    message = packed(current[0], current[1])
    for peer in range(message_ref.shape[0] // rhs):
        message_ref[peer * rhs : (peer + 1) * rhs, :] = message
    for copy in sent:
        copy.wait()


def tables_kernel(
    total_leaves,
    levels,
    dev_ref,
    points_ref,
    charges_ref,
    ordering_ref,
    transfer_ref,
    coupling_ref,
    local_ref,
    pay_right_ref,
    pay_left_ref,
    counts_ref,
    inverse_ref,
    paths_ref,
):
    device = dev_ref[0]
    rhs = charges_ref.shape[0]
    leaves = ordering_ref.shape[0]
    for leaf in range(leaves):
        cols = slice(leaf * LANES, (leaf + 1) * LANES)
        for ref in (pay_right_ref, pay_left_ref):
            ref[leaf * rhs : (leaf + 1) * rhs, :] = charges_ref[:, cols]
            for axis in range(3):
                at = leaves * (rhs + axis) + leaf
                ref[at : at + 1, :] = points_ref[axis : axis + 1, cols]
    for ref, skip in ((pay_right_ref, True), (pay_left_ref, False)):
        edges = []
        base = 0
        for level in range(4):
            count = leaves >> level
            start = base + (count - 3) * rhs if skip else base
            edges.append(local_ref[start : start + 3 * rhs, :].reshape(3, rhs, LANES))
            base += count * rhs
        pairs = paired(jnp.concatenate(edges, axis=0))
        ref[leaves * (rhs + 3) :, :] = pairs.reshape(6 * rhs, LANES)
    slots = lax.broadcasted_iota(jnp.int32, (LANES, LANES), 0)
    numbers = lax.broadcasted_iota(jnp.int32, (16, LANES), 1).astype(jnp.float32)
    numbers = numbers.astype(jnp.bfloat16)
    for leaf in range(leaves):
        hit = jnp.where(ordering_ref[leaf : leaf + 1, :] == slots, 1.0, 0.0).astype(jnp.bfloat16)
        found = bf16_dot(numbers, hit, ((1,), (1,)))
        inverse_ref[leaf : leaf + 1, :] = found[0:1].astype(jnp.int32)
    path = up_matrix(transfer_ref)
    for level in range(5, TOP + 1):
        paths_ref[:, (level - 5) * LANES : (level - 4) * LANES] = path
        if level < TOP:
            bit = ((device % GROUP) >> (level - 5)) & 1
            path = dot(path[:, : LANES // 2], twice(transfer_ref[bit]))
    lane = lax.broadcasted_iota(jnp.int32, (1, LANES), 1)
    starts = level_starts(total_leaves, levels)
    last = starts[-1] // LANES * LANES
    width = coupling_ref.shape[1] - last
    for level in range(levels):
        clusters = total_leaves >> level
        if starts[level] >= last:
            ids = jnp.concatenate(
                [
                    coupling_ref[:, last : last + width],
                    jnp.zeros((coupling_ref.shape[0], LANES - width), jnp.int32),
                ],
                axis=1,
            )
            targets = lane + (last - starts[level])
        else:
            count = leaves >> level if level < 4 else 2 * GROUP >> (level - 4)
            unit = device if level < 4 else device // GROUP
            tile = unit * count // LANES
            ids = coupling_ref[
                :, pl.ds(pl.multiple_of(starts[level] + tile * LANES, LANES), LANES)
            ]
            targets = lane + tile * LANES
        relative = (ids - targets) & (clusters - 1)
        for slot, shift_by in enumerate(OFFSETS):
            hits = jnp.where(relative == (shift_by & (clusters - 1)), 0.5**level, 0.0)
            counts_ref[4 * level + slot : 4 * level + slot + 1, :] = jnp.sum(
                hits, axis=0, keepdims=True
            )


def near_kernel(
    total_leaves, dev_ref, near_in, own_ref, before_ref, after_ref, *rest
):
    out_ref, places, weights, near_ref, arrived = rest[-5:]
    copy = pltpu.make_async_copy(near_in, near_ref, arrived)
    copy.start()
    rhs = out_ref.shape[0]
    leaves = near_in.shape[1]
    entries = near_in.shape[0]
    for part, ref in enumerate((before_ref, own_ref, after_ref)):
        rows = slice(part * leaves, (part + 1) * leaves)
        axes = [
            ref[leaves * (rhs + axis) : leaves * (rhs + axis + 1), :] - 0.5 for axis in range(3)
        ]
        for axis in range(3):
            places[axis, rows, :] = axes[axis]
        places[3, rows, :] = axes[1] * axes[1] + axes[2] * axes[2]

        def fill(leaf, carry, part=part, ref=ref):
            charge = ref[pl.ds(pl.multiple_of(leaf * rhs, rhs), rhs), :] * (0.25 / math.pi)
            weights[part * leaves + leaf] = jnp.concatenate(halves(charge), axis=0)
            return carry

        lax.fori_loop(0, leaves, fill, 0, unroll=8)

    copy.wait()
    device = dev_ref[0]
    half_cycle = total_leaves // 2

    def row_of(kind, slot):
        return places[kind, pl.ds(slot, 1), :]

    def one(leaf, carry):
        target = device * leaves + leaf
        here = [row_of(kind, leaves + leaf) for kind in range(4)]
        size = here[0] * here[0] + (here[3] + DELTA * DELTA)
        table = jnp.concatenate(
            [-2.0 * here[0], -2.0 * here[1], -2.0 * here[2], size]
            + [jnp.zeros((4, LANES), jnp.float32)],
            axis=0,
        )
        columns = jnp.transpose(table)
        ax, ay, az, size = [
            jnp.broadcast_to(columns[:, kind : kind + 1], (LANES, LANES)) for kind in range(4)
        ]
        total = jnp.zeros((2 * rhs, 2 * LANES), jnp.float32)
        for pair in range(entries // 2):
            highs, lows, sides = [], [], []
            for entry in (2 * pair, 2 * pair + 1):
                window = (
                    (near_ref[entry, leaf] - target + half_cycle) & (total_leaves - 1)
                ) - half_cycle
                source = leaves + leaf + window
                qx = row_of(0, source) + window.astype(jnp.float32) * (1.0 / leaves)
                squared = qx * qx + row_of(3, source)
                value = lax.rsqrt(
                    ((size + squared) + ax * qx) + (ay * row_of(1, source) + az * row_of(2, source))
                )
                high, low = halves(value)
                highs.append(high)
                lows.append(low)
                sides.append(weights[source])
            piece = jnp.concatenate(
                [jnp.concatenate(highs, axis=1), jnp.concatenate(lows, axis=1)], axis=0
            )
            total = total + bf16_dot(jnp.concatenate(sides, axis=1), piece, ((1,), (1,)))
        half = total[:, :LANES] + total[:, LANES:]
        out_ref[:, pl.ds(pl.multiple_of(leaf * LANES, LANES), LANES)] = (
            half[0:rhs, :] + half[rhs : 2 * rhs, :]
        )
        return carry

    lax.fori_loop(0, leaves, one, 0, unroll=16)


def couple(window, count, level, lane0, counts_ref, x_ref, row0, rows):
    for t in range(count):
        parts = [
            window(t + shift_by, slot) * counts_ref[4 * level + slot, lane0 + t]
            for slot, shift_by in enumerate(OFFSETS)
        ]
        where = slice(row0 + t * rows, row0 + (t + 1) * rows)
        x_ref[where, 0:LANES] = packed(parts[0], parts[1])
        x_ref[where, LANES : 2 * LANES] = packed(parts[2], parts[3])


def local_kernel(
    dev_ref,
    counts_in,
    local_ref,
    before_ref,
    after_ref,
    stack_ref,
    out_ref,
    x_ref,
    edge_ref,
    counts_ref,
    arrived,
):
    copy = pltpu.make_async_copy(counts_in, counts_ref, arrived)
    copy.start()
    device = dev_ref[0]
    rhs = local_ref.shape[0] // 60
    start = before_ref.shape[0] - 6 * rhs
    for side, ref in enumerate((before_ref, after_ref)):
        for pair in range(6):
            both = ref[start + pair * rhs : start + (pair + 1) * rhs, :]
            edge_ref[side, 2 * pair], edge_ref[side, 2 * pair + 1] = unpacked(both)
    copy.wait()
    base = 0
    for level in range(4):
        count = 32 >> level

        def window(t, slot, count=count, base=base, level=level):
            if t < 0:
                return edge_ref[0, 3 * level + t + 3]
            if t >= count:
                return edge_ref[1, 3 * level + t - count]
            return local_ref[base + t * rhs : base + (t + 1) * rhs, :]

        lane0 = (device * count) & (LANES - 1)
        couple(window, count, level, lane0, counts_ref, x_ref, base, rhs)
        base += count * rhs
    terms = dot(x_ref[...], stack_ref[...])
    out_ref[...] = paired(terms.reshape(-1, rhs, LANES)).reshape(out_ref.shape)


def upper_kernel(
    total_leaves,
    levels,
    dev_ref,
    counts_in,
    gathered_ref,
    transfer_ref,
    stack_ref,
    paths_ref,
    out_ref,
    x_ref,
    top_ref,
    counts_ref,
    arrived,
    *sparse,
):
    copy = pltpu.make_async_copy(counts_in, counts_ref, arrived)
    copy.start()
    device = dev_ref[0]
    index = device % GROUP
    group = device // GROUP
    rhs = out_ref.shape[0] // GROUP
    groups = gathered_ref.shape[0] // rhs
    matrix = up_matrix(transfer_ref)
    half = LANES // 2

    current = dot(gathered_ref[...], paths_ref[:, (TOP - 5) * LANES :]).reshape(groups, rhs, LANES)
    base = 0
    for level in range(TOP, levels):
        top_ref[base : base + current.shape[0]] = current
        base += current.shape[0]
        if level < levels - 1:
            current = up(current, matrix)

    beside = [
        gathered_ref[pl.ds(pl.multiple_of(((group + step) & (groups - 1)) * rhs, 8), rhs), :]
        for step in range(-2, 3)
    ]
    for ref in sparse:
        ref[...] = jnp.zeros(ref.shape, jnp.float32)

    def place(ref, count, position, value):
        inside = (position >= -3) & (position < count + 3)
        ref[jnp.where(inside, position + 3, count + 6)] = value

    for step in (-1, 0, 1):
        for side, value in enumerate(unpacked(beside[step + 2])):
            place(sparse[0], 2 * GROUP, step * 2 * GROUP + 2 * index + side, value)
    nearby = dot(jnp.concatenate(beside, axis=0), paths_ref[:, : (TOP - 5) * LANES])
    for level in range(5, TOP):
        count = 2 * GROUP >> (level - 4)
        reach = (-1, 0, 1) if count >= 3 else (-2, -1, 0, 1, 2)
        for step in reach:
            place(
                sparse[level - 4],
                count,
                step * count + (index >> (level - 5)),
                nearby[(step + 2) * rhs : (step + 3) * rhs, (level - 5) * LANES :][:, :LANES],
            )

    starts = level_starts(total_leaves, levels)
    last = starts[-1] // LANES * LANES

    def lane_of(level, cluster):
        return cluster + starts[level] - last if starts[level] >= last else cluster & (LANES - 1)

    copy.wait()
    row0 = 0
    spans = []
    for level in range(4, TOP):
        count = 2 * GROUP >> (level - 4)
        ref = sparse[level - 4]
        lane0 = lane_of(level, group * count)
        couple(
            lambda t, slot, ref=ref: ref[t + 3], count, level, lane0, counts_ref, x_ref, row0, rhs
        )
        spans.append((row0, count))
        row0 += count * rhs
    top_base = 0
    for level in range(TOP, levels):
        clusters = groups >> (level - TOP)
        cluster = group >> (level - TOP)
        couple(
            lambda t, slot: top_ref[top_base + ((cluster + t) & (clusters - 1))],
            1,
            level,
            lane_of(level, cluster),
            counts_ref,
            x_ref,
            row0,
            rhs,
        )
        spans.append((row0, 1))
        row0 += rhs
        top_base += clusters
    terms = dot(x_ref[...], stack_ref[...])

    def term(level):
        start, count = spans[level - 4]
        return terms[start : start + count * rhs].reshape(count, rhs, LANES)

    current = term(levels - 1)[0]
    for level in range(levels - 2, TOP - 1, -1):
        child = (group >> (level - TOP)) & 1
        current = term(level)[0] + down(current, transfer_ref[child])
    both = jnp.concatenate([transfer_ref[0], transfer_ref[1]], axis=0)
    current = (dot_t(current[:, :half], both) + paired(term(TOP - 1))[0])[None]
    matrix = down_matrix(transfer_ref)
    for level in range(TOP - 2, 3, -1):
        current = paired(term(level)) + down_pairs(current, matrix)
    out_ref[...] = current.reshape(out_ref.shape)


def final_kernel(
    parts_ref, terms_ref, transfer_ref, basis_ref, inverse_ref, near_ref, out_ref
):
    rhs = out_ref.shape[0]
    leaves = inverse_ref.shape[0]
    total = parts_ref[0:rhs, :]
    for sender in range(1, GROUP):
        total = total + parts_ref[sender * rhs : (sender + 1) * rhs, :]
    current = total[None]
    matrix = down_matrix(transfer_ref)
    base = terms_ref.shape[0]
    for level in (3, 2, 1, 0):
        count = leaves >> level + 1
        base -= count * rhs
        mine = terms_ref[base : base + count * rhs, :].reshape(count, rhs, LANES)
        current = mine + down_pairs(current, matrix)
    lane = lax.broadcasted_iota(jnp.int32, (rhs, LANES), 1)
    low = lane < LANES // 2
    zero = jnp.zeros((rhs, LANES), jnp.float32)
    for four in range(leaves // 4):
        rows, sides = [], []
        for slot in range(4):
            leaf = 4 * four + slot
            value = jnp.where(low if slot % 2 == 0 else ~low, current[leaf // 2], 0.0)
            rows.append(jnp.concatenate([value, zero] if slot < 2 else [zero, value], axis=1))
            sides.append(basis_ref[:, leaf * LANES : (leaf + 1) * LANES])
        far = dot(jnp.concatenate(rows, axis=0), jnp.concatenate(sides, axis=0))
        for slot in range(4):
            leaf = 4 * four + slot
            ids = jnp.broadcast_to(inverse_ref[leaf : leaf + 1, :], (rhs, LANES))
            value = jnp.take_along_axis(far[slot * rhs : (slot + 1) * rhs], ids, axis=1)
            cols = slice(leaf * LANES, (leaf + 1) * LANES)
            out_ref[:, cols] = value + near_ref[:, cols]


def call(kernel, outs, scalars, operands, scratch=(), cost=None, kept=(), limit=VMEM_BYTES, far=0):
    smem = pl.BlockSpec(memory_space=pltpu.SMEM)
    vmem = pl.BlockSpec(memory_space=pltpu.VMEM)
    hbm = pl.BlockSpec(memory_space=pltpu.HBM)
    return pl.pallas_call(
        kernel,
        out_shape=outs,
        in_specs=[smem] * len(scalars) + [vmem] * len(operands) + [hbm] * len(kept),
        out_specs=[hbm] * far + [vmem] * (len(outs) - far) if isinstance(outs, list) else vmem,
        scratch_shapes=list(scratch),
        cost_estimate=cost,
        compiler_params=pltpu.CompilerParams(vmem_limit_bytes=limit),
    )(*scalars, *operands, *kept)


def local(points, charges, basis, transfer, near_list, coupling_list, ordering):
    devices = lax.axis_size("leaf")
    device = jnp.reshape(lax.axis_index("leaf"), (1,)).astype(jnp.int32)
    leaves = near_list.shape[1]
    rhs = charges.shape[0]
    total_leaves = leaves * devices
    levels = total_leaves.bit_length() - 3
    groups = devices // GROUP
    f32 = jnp.float32
    ids = ordering.reshape(leaves, LANES)
    stack = jnp.asarray(coupling_stack())
    pay_rows = leaves * (rhs + 3) + 6 * rhs
    local_rows = (leaves * 2 - 4) * rhs

    inputs = [charges, ids, basis, transfer]
    local_terms, message = call(
        expand_kernel,
        [
            jax.ShapeDtypeStruct((local_rows, LANES), f32),
            jax.ShapeDtypeStruct((groups * rhs, LANES), f32),
        ],
        [],
        [],
        [
            *[pltpu.VMEM(array.shape, array.dtype) for array in inputs],
            pltpu.VMEM((local_rows, LANES), f32),
            pltpu.SemaphoreType.DMA((len(inputs) + 4,)),
        ],
        kept=inputs,
        limit=FIRST_BYTES,
        far=1,
    )
    pay_right, pay_left, counts, inverse, paths = call(
        lambda *refs: tables_kernel(total_leaves, levels, *refs),
        [
            jax.ShapeDtypeStruct((pay_rows, LANES), f32),
            jax.ShapeDtypeStruct((pay_rows, LANES), f32),
            jax.ShapeDtypeStruct((4 * levels, LANES), f32),
            jax.ShapeDtypeStruct((leaves, LANES), jnp.int32),
            jax.ShapeDtypeStruct((LANES, (TOP - 4) * LANES), f32),
        ],
        [device],
        [points, charges, ids, transfer, coupling_list, local_terms],
        cost=pl.CostEstimate(flops=1 << 28, bytes_accessed=2 << 20, transcendentals=0),
    )
    before = lax.ppermute(pay_right, "leaf", [(i, (i + 1) % devices) for i in range(devices)])
    after = lax.ppermute(pay_left, "leaf", [((i + 1) % devices, i) for i in range(devices)])
    gathered = lax.all_to_all(
        message,
        "leaf",
        0,
        0,
        axis_index_groups=[[g * GROUP + i for g in range(groups)] for i in range(GROUP)],
        tiled=True,
    )

    terms = call(
        local_kernel,
        jax.ShapeDtypeStruct((local_rows // 2, LANES), f32),
        [device],
        [counts, local_terms, before, after, stack],
        [
            pltpu.VMEM((local_rows, 2 * LANES), f32),
            pltpu.VMEM((2, 12, rhs, LANES), f32),
            pltpu.SMEM(counts.shape, f32),
            pltpu.SemaphoreType.DMA,
        ],
    )
    upper_rows = (4 * GROUP - 2 + levels - TOP) * rhs
    spread = call(
        lambda *refs: upper_kernel(total_leaves, levels, *refs),
        jax.ShapeDtypeStruct((GROUP * rhs, LANES), f32),
        [device],
        [counts, gathered, transfer, stack, paths],
        [
            pltpu.VMEM((upper_rows, 2 * LANES), f32),
            pltpu.VMEM((2 * groups, rhs, LANES), f32),
            pltpu.SMEM(counts.shape, f32),
            pltpu.SemaphoreType.DMA,
            *[
                pltpu.VMEM(((2 * GROUP >> step) + 7, rhs, LANES), f32)
                for step in range(TOP - 4)
            ],
        ],
    )
    parts = lax.all_to_all(
        spread,
        "leaf",
        0,
        0,
        axis_index_groups=[[g * GROUP + i for i in range(GROUP)] for g in range(groups)],
        tiled=True,
    )
    near = call(
        lambda *refs: near_kernel(total_leaves, *refs),
        jax.ShapeDtypeStruct((rhs, leaves * LANES), f32),
        [device],
        [near_list, pay_right, before, after],
        [
            pltpu.VMEM((4, 3 * leaves, LANES), f32),
            pltpu.VMEM((3 * leaves, 2 * rhs, LANES), jnp.bfloat16),
            pltpu.SMEM(near_list.shape, jnp.int32),
            pltpu.SemaphoreType.DMA,
        ],
        pl.CostEstimate(
            flops=leaves * 12 * 128 * 128 * 100,
            bytes_accessed=8 << 20,
            transcendentals=leaves * 12 * 128 * 128,
        ),
        kept=[spread],
    )
    return call(
        final_kernel,
        jax.ShapeDtypeStruct(charges.shape, f32),
        [],
        [parts, terms, transfer, basis, inverse, near],
    )


def solution(mesh):
    placed = (
        P(None, "leaf"),
        P(None, "leaf"),
        P(None, "leaf"),
        P(),
        P(None, "leaf"),
        P(),
        P("leaf"),
    )
    return jax.shard_map(
        local, mesh=mesh, in_specs=placed, out_specs=P(None, "leaf"), check_vma=False
    )
```

```python
import math

import jax
import jax.numpy as jnp
import numpy as np
from jax import lax
from jax.experimental import pallas as pl
from jax.experimental.pallas import tpu as pltpu
from jax.sharding import PartitionSpec as P

ORDER = 4
OFFSETS = (2, 3, -3, -2)
DELTA = 0.05
PROXY = 0.35
GROUP = 16
LANES = 128
TOP = GROUP.bit_length() + 4
VMEM_BYTES = 50 * 1024 * 1024
FIRST_BYTES = 61 * 1024 * 1024


def coupling_stack():
    nodes = np.cos((2.0 * np.arange(ORDER) + 1.0) * (math.pi / (2.0 * ORDER)))
    grid = np.stack(np.meshgrid(nodes, nodes, nodes, indexing="ij")).reshape(3, -1) * PROXY
    stacked = []
    for shift_by in OFFSETS:
        moved = grid + np.array([float(shift_by), 0.0, 0.0])[:, None]
        difference = grid[:, :, None] - moved[:, None, :]
        stacked.append((0.25 / math.pi / np.sqrt((difference**2).sum(0))).T)
    table = np.concatenate(stacked, axis=0)
    return np.concatenate([table, table], axis=1).astype(np.float32)


def halves(value):
    high = value.astype(jnp.bfloat16)
    return high, (value - high.astype(jnp.float32)).astype(jnp.bfloat16)


def bf16_dot(left, right, dims):
    return lax.dot_general(left, right, (dims, ((), ())), preferred_element_type=jnp.float32)


def summed(product, rows, columns):
    return product[:rows, :columns] + (product[:rows, columns:] + product[rows:, :columns])


def dot(left, right):
    both = bf16_dot(
        jnp.concatenate(halves(left), axis=0), jnp.concatenate(halves(right), axis=1), ((1,), (0,))
    )
    return summed(both, left.shape[0], right.shape[1])


def dot_t(left, right):
    both = bf16_dot(
        jnp.concatenate(halves(left), axis=0), jnp.concatenate(halves(right), axis=0), ((1,), (1,))
    )
    return summed(both, left.shape[0], right.shape[0])


def first_half(shape):
    return lax.broadcasted_iota(jnp.int32, shape, len(shape) - 1) < LANES // 2


def packed(left, right):
    return jnp.where(first_half(left.shape), left, right)


def unpacked(both):
    turned = pltpu.roll(both, LANES // 2, 1)
    return packed(both, turned), packed(turned, both)


def twice(matrix):
    return jnp.concatenate([matrix, matrix], axis=1)


def up_matrix(transfer_ref):
    return jnp.concatenate([twice(transfer_ref[0]), twice(transfer_ref[1])], axis=0)


def up(values, matrix):
    count, rows, lanes = values.shape
    both = paired(values).reshape(count // 2 * rows, lanes)
    return dot(both, matrix).reshape(count // 2, rows, lanes)


def down(parent, matrix):
    doubled = jnp.concatenate([matrix, matrix], axis=0)
    return dot_t(parent[:, : LANES // 2], doubled)


def down_matrix(transfer_ref):
    both = jnp.concatenate([transfer_ref[0], transfer_ref[1]], axis=0)
    zero = jnp.zeros(both.shape, jnp.float32)
    return jnp.concatenate(
        [jnp.concatenate([both, zero], axis=1), jnp.concatenate([zero, both], axis=1)], axis=0
    )


def down_pairs(pairs, matrix):
    count, rows, lanes = pairs.shape
    both = dot_t(pairs.reshape(count * rows, lanes), matrix).reshape(count, rows, 2 * lanes)
    return jnp.stack([both[:, :, :lanes], both[:, :, lanes:]], axis=1).reshape(
        2 * count, rows, lanes
    )


def paired(values):
    count, rows, lanes = values.shape
    pairs = values.reshape(count // 2, 2, rows, lanes)
    return packed(pairs[:, 0], pairs[:, 1])


def level_starts(total_leaves, levels):
    return [2 * total_leaves - 2 * (total_leaves >> level) for level in range(levels)]


def expand_kernel(
    charges_in,
    ordering_in,
    basis_in,
    transfer_in,
    local_out,
    message_ref,
    charges_ref,
    ordering_ref,
    basis_ref,
    transfer_ref,
    local_ref,
    arrived,
):
    moves = [
        (charges_in, charges_ref),
        (ordering_in, ordering_ref),
        (basis_in, basis_ref),
        (transfer_in, transfer_ref),
    ]
    copies = [
        pltpu.make_async_copy(source, target, arrived.at[slot])
        for slot, (source, target) in enumerate(moves)
    ]
    for copy in copies:
        copy.start()
    for copy in copies:
        copy.wait()
    rhs = charges_ref.shape[0]
    leaves = ordering_ref.shape[0]
    zero = jnp.zeros((rhs, LANES), jnp.float32)
    expansions = []
    for pair in range(leaves // 2):
        gathered = []
        for leaf in (2 * pair, 2 * pair + 1):
            ids = jnp.broadcast_to(ordering_ref[leaf : leaf + 1, :], (rhs, LANES))
            cols = slice(leaf * LANES, (leaf + 1) * LANES)
            gathered.append(jnp.take_along_axis(charges_ref[:, cols], ids, axis=1))
        left = jnp.concatenate(
            [
                jnp.concatenate([gathered[0], zero], axis=1),
                jnp.concatenate([zero, gathered[1]], axis=1),
            ],
            axis=0,
        )
        part = basis_ref[:, 2 * pair * LANES : (2 * pair + 2) * LANES]
        both = dot_t(left, jnp.concatenate([part, part], axis=0))
        expansions.append(both.reshape(2, rhs, LANES))
    current = jnp.concatenate(expansions, axis=0)
    local_ref[...] = current.reshape(local_ref.shape)
    sent = pltpu.make_async_copy(local_ref, local_out, arrived.at[len(moves)])
    sent.start()
    one = jnp.concatenate([transfer_ref[0], transfer_ref[1]], axis=0)
    two = dot(one, jnp.concatenate([transfer_ref[0], transfer_ref[1]], axis=1))
    half = LANES // 2
    quarters = [
        two[low * half : (low + 1) * half, high * half : (high + 1) * half]
        for high in range(2)
        for low in range(2)
    ]
    four = dot(jnp.concatenate(quarters, axis=0), jnp.concatenate(quarters, axis=1))
    path = jnp.concatenate([four[:, k * half : (k + 1) * half] for k in range(4)], axis=0)
    pairs = paired(current).reshape(2, leaves // 4, rhs, LANES)
    rows = jnp.concatenate([pairs[:, k] for k in range(leaves // 4)], axis=2)
    above = dot(rows.reshape(2 * rhs, leaves // 4 * LANES), twice(path))
    message = packed(above[:rhs], above[rhs:])
    for peer in range(message_ref.shape[0] // rhs):
        message_ref[peer * rhs : (peer + 1) * rhs, :] = message
    sent.wait()


def payload_kernel(
    points_ref,
    charges_ref,
    transfer_ref,
    lowest_ref,
    _,
    pay_right_ref,
    pay_left_ref,
    local_ref,
):
    rhs = charges_ref.shape[0]
    leaves = charges_ref.shape[1] // LANES
    for leaf in range(leaves):
        cols = slice(leaf * LANES, (leaf + 1) * LANES)
        for ref in (pay_right_ref, pay_left_ref):
            ref[leaf * rhs : (leaf + 1) * rhs, :] = charges_ref[:, cols]
            for axis in range(3):
                at = leaves * (rhs + axis) + leaf
                ref[at : at + 1, :] = points_ref[axis : axis + 1, cols]
    current = lowest_ref[...].reshape(leaves, rhs, LANES)
    matrix = up_matrix(transfer_ref)
    base = 0
    lasts, firsts = [], []
    for level in range(4):
        count = leaves >> level
        local_ref[base : base + count * rhs, :] = current.reshape(count * rhs, LANES)
        lasts.append(current[count - 3 :])
        firsts.append(current[:3])
        base += count * rhs
        if level < 3:
            current = up(current, matrix)
    for ref, edges in ((pay_right_ref, lasts), (pay_left_ref, firsts)):
        pairs = paired(jnp.concatenate(edges, axis=0))
        ref[leaves * (rhs + 3) :, :] = pairs.reshape(6 * rhs, LANES)


def tables_kernel(
    total_leaves,
    levels,
    dev_ref,
    ordering_ref,
    transfer_ref,
    coupling_ref,
    _,
    counts_ref,
    inverse_ref,
    paths_ref,
):
    device = dev_ref[0]
    leaves = ordering_ref.shape[0]
    slots = lax.broadcasted_iota(jnp.int32, (LANES, LANES), 0)
    numbers = lax.broadcasted_iota(jnp.int32, (16, LANES), 1).astype(jnp.float32)
    numbers = numbers.astype(jnp.bfloat16)
    for leaf in range(leaves):
        hit = jnp.where(ordering_ref[leaf : leaf + 1, :] == slots, 1.0, 0.0).astype(jnp.bfloat16)
        found = bf16_dot(numbers, hit, ((1,), (1,)))
        inverse_ref[leaf : leaf + 1, :] = found[0:1].astype(jnp.int32)
    path = up_matrix(transfer_ref)
    for level in range(5, TOP + 1):
        paths_ref[:, (level - 5) * LANES : (level - 4) * LANES] = path
        if level < TOP:
            bit = ((device % GROUP) >> (level - 5)) & 1
            path = dot(path[:, : LANES // 2], twice(transfer_ref[bit]))
    lane = lax.broadcasted_iota(jnp.int32, (1, LANES), 1)
    starts = level_starts(total_leaves, levels)
    last = starts[-1] // LANES * LANES
    width = coupling_ref.shape[1] - last
    for level in range(levels):
        clusters = total_leaves >> level
        if starts[level] >= last:
            ids = jnp.concatenate(
                [
                    coupling_ref[:, last : last + width],
                    jnp.zeros((coupling_ref.shape[0], LANES - width), jnp.int32),
                ],
                axis=1,
            )
            targets = lane + (last - starts[level])
        else:
            count = leaves >> level if level < 4 else 2 * GROUP >> (level - 4)
            unit = device if level < 4 else device // GROUP
            tile = unit * count // LANES
            ids = coupling_ref[
                :, pl.ds(pl.multiple_of(starts[level] + tile * LANES, LANES), LANES)
            ]
            targets = lane + tile * LANES
        relative = (ids - targets) & (clusters - 1)
        for slot, shift_by in enumerate(OFFSETS):
            hits = jnp.where(relative == (shift_by & (clusters - 1)), 0.5**level, 0.0)
            counts_ref[4 * level + slot : 4 * level + slot + 1, :] = jnp.sum(
                hits, axis=0, keepdims=True
            )


def inverse_distance(table, squared, qx, qy, qz):
    columns = jnp.transpose(table)
    ax, ay, az, size = [
        jnp.broadcast_to(columns[:, kind : kind + 1], (LANES, LANES)) for kind in range(4)
    ]
    return lax.rsqrt(((size + squared) + ax * qx) + (ay * qy + az * qz))


def own_kernel(points_ref, charges_ref, _, out_ref):
    rhs = charges_ref.shape[0]
    for leaf in range(charges_ref.shape[1] // LANES):
        cols = slice(leaf * LANES, (leaf + 1) * LANES)
        qx, qy, qz = [points_ref[axis : axis + 1, cols] - 0.5 for axis in range(3)]
        squared = qx * qx + (qy * qy + qz * qz)
        table = jnp.concatenate(
            [-2.0 * qx, -2.0 * qy, -2.0 * qz, squared + DELTA * DELTA]
            + [jnp.zeros((4, LANES), jnp.float32)],
            axis=0,
        )
        value = inverse_distance(table, squared, qx, qy, qz)
        piece = jnp.concatenate(halves(value), axis=0)
        side = jnp.concatenate(halves(charges_ref[:, cols] * (0.25 / math.pi)), axis=0)
        total = bf16_dot(side, piece, ((1,), (1,)))
        half = total[:, :LANES] + total[:, LANES:]
        out_ref[:, cols] = half[0:rhs, :] + half[rhs : 2 * rhs, :]


def near_kernel(
    total_leaves, dev_ref, near_in, own_ref, before_ref, after_ref, itself_ref, *rest
):
    out_ref, places, weights, near_ref, arrived = rest[-5:]
    copy = pltpu.make_async_copy(near_in, near_ref, arrived)
    copy.start()
    rhs = out_ref.shape[0]
    leaves = near_in.shape[1]
    entries = near_in.shape[0]
    for part, ref in enumerate((before_ref, own_ref, after_ref)):
        rows = slice(part * leaves, (part + 1) * leaves)
        axes = [
            ref[leaves * (rhs + axis) : leaves * (rhs + axis + 1), :] - 0.5 for axis in range(3)
        ]
        for axis in range(3):
            places[axis, rows, :] = axes[axis]
        places[3, rows, :] = axes[1] * axes[1] + axes[2] * axes[2]

        def fill(leaf, carry, part=part, ref=ref):
            charge = ref[pl.ds(pl.multiple_of(leaf * rhs, rhs), rhs), :] * (0.25 / math.pi)
            weights[part * leaves + leaf] = jnp.concatenate(halves(charge), axis=0)
            return carry

        lax.fori_loop(0, leaves, fill, 0, unroll=8)

    copy.wait()
    device = dev_ref[0]
    half_cycle = total_leaves // 2

    def row_of(kind, slot):
        return places[kind, pl.ds(slot, 1), :]

    def one(leaf, carry):
        target = device * leaves + leaf
        here = [row_of(kind, leaves + leaf) for kind in range(4)]
        size = here[0] * here[0] + (here[3] + DELTA * DELTA)
        table = jnp.concatenate(
            [-2.0 * here[0], -2.0 * here[1], -2.0 * here[2], size]
            + [jnp.zeros((4, LANES), jnp.float32)],
            axis=0,
        )
        columns = jnp.transpose(table)
        ax, ay, az, size = [
            jnp.broadcast_to(columns[:, kind : kind + 1], (LANES, LANES)) for kind in range(4)
        ]
        total = jnp.zeros((2 * rhs, 2 * LANES), jnp.float32)
        for pair in range(entries // 2):
            highs, lows, sides = [], [], []
            for entry in range(2 * pair + 1, min(2 * pair + 3, entries)):
                window = (
                    (near_ref[entry, leaf] - target + half_cycle) & (total_leaves - 1)
                ) - half_cycle
                source = leaves + leaf + window
                qx = row_of(0, source) + window.astype(jnp.float32) * (1.0 / leaves)
                squared = qx * qx + row_of(3, source)
                value = lax.rsqrt(
                    ((size + squared) + ax * qx) + (ay * row_of(1, source) + az * row_of(2, source))
                )
                high, low = halves(value)
                highs.append(high)
                lows.append(low)
                sides.append(weights[source])
            piece = jnp.concatenate(
                [jnp.concatenate(highs, axis=1), jnp.concatenate(lows, axis=1)], axis=0
            )
            total = total + bf16_dot(jnp.concatenate(sides, axis=1), piece, ((1,), (1,)))
        half = total[:, :LANES] + total[:, LANES:]
        cols = pl.ds(pl.multiple_of(leaf * LANES, LANES), LANES)
        out_ref[:, cols] = itself_ref[:, cols] + (half[0:rhs, :] + half[rhs : 2 * rhs, :])
        return carry

    lax.fori_loop(0, leaves, one, 0, unroll=16)


def couple(window, count, level, lane0, counts_ref, x_ref, row0, rows):
    for t in range(count):
        parts = [
            window(t + shift_by, slot) * counts_ref[4 * level + slot, lane0 + t]
            for slot, shift_by in enumerate(OFFSETS)
        ]
        where = slice(row0 + t * rows, row0 + (t + 1) * rows)
        x_ref[where, 0:LANES] = packed(parts[0], parts[1])
        x_ref[where, LANES : 2 * LANES] = packed(parts[2], parts[3])


def local_kernel(
    dev_ref,
    counts_in,
    local_ref,
    before_ref,
    after_ref,
    stack_ref,
    out_ref,
    x_ref,
    edge_ref,
    counts_ref,
    arrived,
):
    copy = pltpu.make_async_copy(counts_in, counts_ref, arrived)
    copy.start()
    device = dev_ref[0]
    rhs = local_ref.shape[0] // 60
    start = before_ref.shape[0] - 6 * rhs
    for side, ref in enumerate((before_ref, after_ref)):
        for pair in range(6):
            both = ref[start + pair * rhs : start + (pair + 1) * rhs, :]
            edge_ref[side, 2 * pair], edge_ref[side, 2 * pair + 1] = unpacked(both)
    copy.wait()
    base = 0
    for level in range(4):
        count = 32 >> level

        def window(t, slot, count=count, base=base, level=level):
            if t < 0:
                return edge_ref[0, 3 * level + t + 3]
            if t >= count:
                return edge_ref[1, 3 * level + t - count]
            return local_ref[base + t * rhs : base + (t + 1) * rhs, :]

        lane0 = (device * count) & (LANES - 1)
        couple(window, count, level, lane0, counts_ref, x_ref, base, rhs)
        base += count * rhs
    terms = dot(x_ref[...], stack_ref[...])
    out_ref[...] = paired(terms.reshape(-1, rhs, LANES)).reshape(out_ref.shape)


def upper_kernel(
    total_leaves,
    levels,
    dev_ref,
    counts_in,
    gathered_ref,
    transfer_ref,
    stack_ref,
    paths_ref,
    _,
    out_ref,
    x_ref,
    top_ref,
    counts_ref,
    arrived,
    *sparse,
):
    copy = pltpu.make_async_copy(counts_in, counts_ref, arrived)
    copy.start()
    device = dev_ref[0]
    index = device % GROUP
    group = device // GROUP
    rhs = out_ref.shape[0] // GROUP
    groups = gathered_ref.shape[0] // rhs
    matrix = up_matrix(transfer_ref)
    half = LANES // 2

    current = dot(gathered_ref[...], paths_ref[:, (TOP - 5) * LANES :]).reshape(groups, rhs, LANES)
    base = 0
    for level in range(TOP, levels):
        top_ref[base : base + current.shape[0]] = current
        base += current.shape[0]
        if level < levels - 1:
            current = up(current, matrix)

    beside = [
        gathered_ref[pl.ds(pl.multiple_of(((group + step) & (groups - 1)) * rhs, 8), rhs), :]
        for step in range(-2, 3)
    ]
    for ref in sparse:
        ref[...] = jnp.zeros(ref.shape, jnp.float32)

    def place(ref, count, position, value):
        inside = (position >= -3) & (position < count + 3)
        ref[jnp.where(inside, position + 3, count + 6)] = value

    for step in (-1, 0, 1):
        for side, value in enumerate(unpacked(beside[step + 2])):
            place(sparse[0], 2 * GROUP, step * 2 * GROUP + 2 * index + side, value)
    nearby = dot(jnp.concatenate(beside, axis=0), paths_ref[:, : (TOP - 5) * LANES])
    for level in range(5, TOP):
        count = 2 * GROUP >> (level - 4)
        reach = (-1, 0, 1) if count >= 3 else (-2, -1, 0, 1, 2)
        for step in reach:
            place(
                sparse[level - 4],
                count,
                step * count + (index >> (level - 5)),
                nearby[(step + 2) * rhs : (step + 3) * rhs, (level - 5) * LANES :][:, :LANES],
            )

    starts = level_starts(total_leaves, levels)
    last = starts[-1] // LANES * LANES

    def lane_of(level, cluster):
        return cluster + starts[level] - last if starts[level] >= last else cluster & (LANES - 1)

    copy.wait()
    row0 = 0
    spans = []
    for level in range(4, TOP):
        count = 2 * GROUP >> (level - 4)
        ref = sparse[level - 4]
        lane0 = lane_of(level, group * count)
        couple(
            lambda t, slot, ref=ref: ref[t + 3], count, level, lane0, counts_ref, x_ref, row0, rhs
        )
        spans.append((row0, count))
        row0 += count * rhs
    top_base = 0
    for level in range(TOP, levels):
        clusters = groups >> (level - TOP)
        cluster = group >> (level - TOP)
        couple(
            lambda t, slot: top_ref[top_base + ((cluster + t) & (clusters - 1))],
            1,
            level,
            lane_of(level, cluster),
            counts_ref,
            x_ref,
            row0,
            rhs,
        )
        spans.append((row0, 1))
        row0 += rhs
        top_base += clusters
    terms = dot(x_ref[...], stack_ref[...])

    def term(level):
        start, count = spans[level - 4]
        return terms[start : start + count * rhs].reshape(count, rhs, LANES)

    current = term(levels - 1)[0]
    for level in range(levels - 2, TOP - 1, -1):
        child = (group >> (level - TOP)) & 1
        current = term(level)[0] + down(current, transfer_ref[child])
    both = jnp.concatenate([transfer_ref[0], transfer_ref[1]], axis=0)
    current = (dot_t(current[:, :half], both) + paired(term(TOP - 1))[0])[None]
    matrix = down_matrix(transfer_ref)
    for level in range(TOP - 2, 3, -1):
        current = paired(term(level)) + down_pairs(current, matrix)
    out_ref[...] = current.reshape(out_ref.shape)


def final_kernel(
    parts_ref, terms_ref, transfer_ref, basis_ref, inverse_ref, near_ref, out_ref
):
    rhs = out_ref.shape[0]
    leaves = inverse_ref.shape[0]
    total = parts_ref[0:rhs, :]
    for sender in range(1, GROUP):
        total = total + parts_ref[sender * rhs : (sender + 1) * rhs, :]
    current = total[None]
    matrix = down_matrix(transfer_ref)
    base = terms_ref.shape[0]
    for level in (3, 2, 1, 0):
        count = leaves >> level + 1
        base -= count * rhs
        mine = terms_ref[base : base + count * rhs, :].reshape(count, rhs, LANES)
        current = mine + down_pairs(current, matrix)
    lane = lax.broadcasted_iota(jnp.int32, (rhs, LANES), 1)
    low = lane < LANES // 2
    zero = jnp.zeros((rhs, LANES), jnp.float32)
    for four in range(leaves // 4):
        rows, sides = [], []
        for slot in range(4):
            leaf = 4 * four + slot
            value = jnp.where(low if slot % 2 == 0 else ~low, current[leaf // 2], 0.0)
            rows.append(jnp.concatenate([value, zero] if slot < 2 else [zero, value], axis=1))
            sides.append(basis_ref[:, leaf * LANES : (leaf + 1) * LANES])
        far = dot(jnp.concatenate(rows, axis=0), jnp.concatenate(sides, axis=0))
        for slot in range(4):
            leaf = 4 * four + slot
            ids = jnp.broadcast_to(inverse_ref[leaf : leaf + 1, :], (rhs, LANES))
            value = jnp.take_along_axis(far[slot * rhs : (slot + 1) * rhs], ids, axis=1)
            cols = slice(leaf * LANES, (leaf + 1) * LANES)
            out_ref[:, cols] = value + near_ref[:, cols]


def call(kernel, outs, scalars, operands, scratch=(), cost=None, kept=(), limit=VMEM_BYTES, far=0):
    smem = pl.BlockSpec(memory_space=pltpu.SMEM)
    vmem = pl.BlockSpec(memory_space=pltpu.VMEM)
    hbm = pl.BlockSpec(memory_space=pltpu.HBM)
    anywhere = pl.BlockSpec(memory_space=pl.ANY)
    return pl.pallas_call(
        kernel,
        out_shape=outs,
        in_specs=[smem] * len(scalars) + [vmem] * len(operands) + [anywhere] * len(kept),
        out_specs=[hbm] * far + [vmem] * (len(outs) - far) if isinstance(outs, list) else vmem,
        scratch_shapes=list(scratch),
        cost_estimate=cost,
        compiler_params=pltpu.CompilerParams(vmem_limit_bytes=limit),
    )(*scalars, *operands, *kept)


def local(points, charges, basis, transfer, near_list, coupling_list, ordering):
    devices = lax.axis_size("leaf")
    device = jnp.reshape(lax.axis_index("leaf"), (1,)).astype(jnp.int32)
    leaves = near_list.shape[1]
    rhs = charges.shape[0]
    total_leaves = leaves * devices
    levels = total_leaves.bit_length() - 3
    groups = devices // GROUP
    f32 = jnp.float32
    ids = ordering.reshape(leaves, LANES)
    stack = jnp.asarray(coupling_stack())
    pay_rows = leaves * (rhs + 3) + 6 * rhs
    local_rows = (leaves * 2 - 4) * rhs

    inputs = [charges, ids, basis, transfer]
    lowest, message = call(
        expand_kernel,
        [
            jax.ShapeDtypeStruct((leaves * rhs, LANES), f32),
            jax.ShapeDtypeStruct((groups * rhs, LANES), f32),
        ],
        [],
        [],
        [
            *[pltpu.VMEM(array.shape, array.dtype) for array in inputs],
            pltpu.VMEM((leaves * rhs, LANES), f32),
            pltpu.SemaphoreType.DMA((len(inputs) + 1,)),
        ],
        kept=inputs,
        limit=FIRST_BYTES,
        far=1,
    )
    counts, inverse, paths = call(
        lambda *refs: tables_kernel(total_leaves, levels, *refs),
        [
            jax.ShapeDtypeStruct((4 * levels, LANES), f32),
            jax.ShapeDtypeStruct((leaves, LANES), jnp.int32),
            jax.ShapeDtypeStruct((LANES, (TOP - 4) * LANES), f32),
        ],
        [device],
        [ids, transfer, coupling_list],
        cost=pl.CostEstimate(flops=1 << 28, bytes_accessed=2 << 20, transcendentals=0),
        kept=[message],
    )
    pay_right, pay_left, local_terms = call(
        payload_kernel,
        [
            jax.ShapeDtypeStruct((pay_rows, LANES), f32),
            jax.ShapeDtypeStruct((pay_rows, LANES), f32),
            jax.ShapeDtypeStruct((local_rows, LANES), f32),
        ],
        [],
        [points, charges, transfer, lowest],
        cost=pl.CostEstimate(flops=1 << 28, bytes_accessed=2 << 20, transcendentals=0),
        kept=[paths],
    )
    itself = call(
        own_kernel,
        jax.ShapeDtypeStruct(charges.shape, f32),
        [],
        [points, charges],
        cost=pl.CostEstimate(
            flops=leaves * 128 * 128 * 100, bytes_accessed=1 << 20, transcendentals=0
        ),
        kept=[local_terms],
    )
    before = lax.ppermute(pay_right, "leaf", [(i, (i + 1) % devices) for i in range(devices)])
    after = lax.ppermute(pay_left, "leaf", [((i + 1) % devices, i) for i in range(devices)])
    gathered = lax.all_to_all(
        message,
        "leaf",
        0,
        0,
        axis_index_groups=[[g * GROUP + i for g in range(groups)] for i in range(GROUP)],
        tiled=True,
    )

    terms = call(
        local_kernel,
        jax.ShapeDtypeStruct((local_rows // 2, LANES), f32),
        [device],
        [counts, local_terms, before, after, stack],
        [
            pltpu.VMEM((local_rows, 2 * LANES), f32),
            pltpu.VMEM((2, 12, rhs, LANES), f32),
            pltpu.SMEM(counts.shape, f32),
            pltpu.SemaphoreType.DMA,
        ],
    )
    upper_rows = (4 * GROUP - 2 + levels - TOP) * rhs
    spread = call(
        lambda *refs: upper_kernel(total_leaves, levels, *refs),
        jax.ShapeDtypeStruct((GROUP * rhs, LANES), f32),
        [device],
        [counts, gathered, transfer, stack, paths],
        [
            pltpu.VMEM((upper_rows, 2 * LANES), f32),
            pltpu.VMEM((2 * groups, rhs, LANES), f32),
            pltpu.SMEM(counts.shape, f32),
            pltpu.SemaphoreType.DMA,
            *[
                pltpu.VMEM(((2 * GROUP >> step) + 7, rhs, LANES), f32)
                for step in range(TOP - 4)
            ],
        ],
        kept=[itself],
    )
    parts = lax.all_to_all(
        spread,
        "leaf",
        0,
        0,
        axis_index_groups=[[g * GROUP + i for i in range(GROUP)] for g in range(groups)],
        tiled=True,
    )
    near = call(
        lambda *refs: near_kernel(total_leaves, *refs),
        jax.ShapeDtypeStruct((rhs, leaves * LANES), f32),
        [device],
        [near_list, pay_right, before, after, itself],
        [
            pltpu.VMEM((4, 3 * leaves, LANES), f32),
            pltpu.VMEM((3 * leaves, 2 * rhs, LANES), jnp.bfloat16),
            pltpu.SMEM(near_list.shape, jnp.int32),
            pltpu.SemaphoreType.DMA,
        ],
        pl.CostEstimate(
            flops=leaves * 12 * 128 * 128 * 100,
            bytes_accessed=8 << 20,
            transcendentals=leaves * 12 * 128 * 128,
        ),
        kept=[spread],
    )
    return call(
        final_kernel,
        jax.ShapeDtypeStruct(charges.shape, f32),
        [],
        [parts, terms, transfer, basis, inverse, near],
    )


def solution(mesh):
    placed = (
        P(None, "leaf"),
        P(None, "leaf"),
        P(None, "leaf"),
        P(),
        P(None, "leaf"),
        P(),
        P("leaf"),
    )
    return jax.shard_map(
        local, mesh=mesh, in_specs=placed, out_specs=P(None, "leaf"), check_vma=False
    )
```
